32 devices in a mesh: px: 4 (over x, core), py: 8 (over z, y).
Axes of the slice: x: 2, y: 2, z: 4, core: 2. Of those that a mesh axis runs over, the one named last changes fastest.
Arguments:
- centroids: float32 [3, 524288], P(None, ('px', 'py')), may hold values from 0 to 3
- volumes: float32 [524288], P(('px', 'py')), may hold values from 0.3 to 3
- densities: float32 [524288], P(('px', 'py')), may hold values from 0.01 to 1
- sens_in: float32 [524288], P(('px', 'py')), may hold values from -192 to 192
- local_first: int32 [2048], P(('px', 'py')), may hold values from 0 to 62, as said below
- local_second: int32 [2048], P(('px', 'py')), may hold values from 1 to 63, as said below
- pair_count: int32 [32, 32], P(('px', 'py')), may hold values from 0 to 4, as said below
- pair_mine: int32 [32, 32, 4], P(('px', 'py')), may hold values from 0 to 63, as said below
Outputs:
- filtered: float32 [524288], P(('px', 'py'))
- sensitivity: float32 [524288], P(('px', 'py'))
The draws below stay inside these ranges and needn't reach their ends.
Inputs may be any that keep to these rules, and one draw needn't show every extreme that they name: `pair_count`: Symmetric, zero on the diagonal, 1 to 4 elsewhere; some partition has 4 pairs with every other one. `pair_mine`: the 4 entries for one d and p are distinct; slot s of (d, p) and slot s of (p, d) name the same pair; slots at or past pair_count[d, p] are unused. local_first < local_second; no pair repeats within a partition. `local_second`: as for local_first.
All inputs are finite; a program needn't handle non-finite values.
Results may differ from the reference program's by a relative error of at most 0.004.
Values may be sent and summed in bfloat16 or wider, within the bound.
No kernel may reach another device: no remote copies, remote signals or barrier semaphores. Data moves between devices by JAX's collectives and lax.ppermute only.
A program may use at most 64 MiB of HBM per device.

```python
import math
import jax
import jax.numpy as jnp
import numpy as np
from jax import lax

BLK = 256
NB_DEV = 64
LP = 64
CAP = 4
PARTITIONS = 32
ELEMS = 524288
N_PX = 4
N_PY = 8


def draw_centroids(key, part):
    key = jax.random.fold_in(key, 31)
    key_centre, key_offset = jax.random.split(key, 2)
    blocks = ELEMS // BLK
    centres = 0.95 + 1.1 * jax.random.uniform(key_centre, (3, blocks, 1), jnp.float32)
    offsets = jax.random.uniform(key_offset, (3, blocks, BLK), jnp.float32) - 0.5
    sides = 1.5
    return (centres + sides * offsets).reshape(3, ELEMS).astype(jnp.float32)


def local_pair_table(key):
    key = jax.random.fold_in(key, 21)
    low, high = np.triu_indices(NB_DEV, 1)
    choices_total = low.shape[0]
    scores = jax.random.randint(key, (PARTITIONS, choices_total), 0, 2 ** 20) * choices_total
    scores = scores + jnp.arange(choices_total, dtype=jnp.int32)[None, :]
    column = lax.broadcasted_iota(jnp.int32, (PARTITIONS, choices_total), 1)
    scores = jnp.where(column == 0, -3, scores)
    scores = jnp.where(column == NB_DEV - 2, -2, scores)
    scores = jnp.where(column == choices_total - 1, -1, scores)
    order = jnp.argsort(scores, axis=1)[:, :LP]
    first = jnp.asarray(low, dtype=jnp.int32)[order].reshape(-1)
    second = jnp.asarray(high, dtype=jnp.int32)[order].reshape(-1)
    return (first, second)


def draw_local_first(key, part):
    return local_pair_table(key)[0]


def draw_local_second(key, part):
    return local_pair_table(key)[1]


def draw_pair_count(key, part):
    key = jax.random.fold_in(key, 11)
    key_raw, key_full = jax.random.split(key)
    raw = jax.random.randint(key_raw, (PARTITIONS, PARTITIONS), 1, CAP + 1)
    rows = lax.broadcasted_iota(jnp.int32, (PARTITIONS, PARTITIONS), 0)
    cols = lax.broadcasted_iota(jnp.int32, (PARTITIONS, PARTITIONS), 1)
    mirrored = jnp.where(rows < cols, raw, raw.T)
    busiest = jax.random.randint(key_full, (), 0, PARTITIONS)
    mirrored = jnp.where((rows == busiest) | (cols == busiest), CAP, mirrored)
    return jnp.where(rows == cols, 0, mirrored).astype(jnp.int32)


def draw_pair_mine(key, part):
    key = jax.random.fold_in(key, 12)
    scores = jax.random.randint(key, (PARTITIONS, PARTITIONS, NB_DEV), 0, 2 ** 20) * NB_DEV
    scores = scores + jnp.arange(NB_DEV, dtype=jnp.int32)[None, None, :]
    order = jnp.argsort(scores, axis=2)[:, :, :CAP]
    return order.astype(jnp.int32)


def level_of(stream_key, dims, cuts, low, high):
    gain = 1.0
    for axis_at, shards_of in cuts:
        steps = jax.random.uniform(jax.random.fold_in(jax.random.fold_in(stream_key, 6), axis_at), (shards_of,), jnp.float32, low / len(cuts), high / len(cuts))
        gain = gain * jnp.repeat(jnp.exp(steps), dims[axis_at] // shards_of).reshape((-1,) + (1,) * (len(dims) - 1 - axis_at))
    return gain


def gaussian(own_key, shape, scale, reach, shards=(), kind=jnp.bfloat16):
    drawn = scale * jax.random.normal(own_key, shape, jnp.float32)
    if shards:
        drawn = drawn * level_of(own_key, shape, shards, -0.22, 0.18)
    return jnp.clip(drawn, -reach, reach).astype(kind)


def setup_inputs(seed: int = 0) -> dict:
    streams_of = jax.random.split(jax.random.key(seed), 9)
    centroids = draw_centroids(jax.random.fold_in(streams_of[8], 71), 0)
    volumes = jnp.clip(jnp.exp(math.log(3.0) - 2.3025851 * jax.random.uniform(streams_of[1], (ELEMS,), jnp.float32) ** level_of(streams_of[1], (ELEMS,), ((0, 32),), -0.2, 0.2)), 0.3, 3.0)
    densities = jnp.clip(0.01 + 0.99 * jax.random.uniform(streams_of[2], (ELEMS,), jnp.float32) ** level_of(streams_of[2], (ELEMS,), ((0, 32),), -0.2, 0.2), 0.01, 1.0)
    sens_in = gaussian(streams_of[3], (ELEMS,), 32.0, 192.0, ((0, 32),), jnp.float32)
    local_first = draw_local_first(jax.random.fold_in(streams_of[8], 71), 0)
    local_second = draw_local_second(jax.random.fold_in(streams_of[8], 71), 0)
    pair_count = draw_pair_count(jax.random.fold_in(streams_of[8], 71), 0)
    pair_mine = draw_pair_mine(jax.random.fold_in(streams_of[8], 71), 0)
    return {"centroids": centroids, "volumes": volumes, "densities": densities, "sens_in": sens_in, "local_first": local_first, "local_second": local_second, "pair_count": pair_count, "pair_mine": pair_mine}


radius = 1.0

def tile_weights(first, second):
    gap_x = first[..., 0, :, None] - second[..., 0, None, :]
    gap_y = first[..., 1, :, None] - second[..., 1, None, :]
    gap_z = first[..., 2, :, None] - second[..., 2, None, :]
    spread = jnp.sqrt(gap_x * gap_x + gap_y * gap_y + gap_z * gap_z)
    return jnp.maximum(radius - spread, 0.0).astype(jnp.bfloat16)

def pair_sums(cent, values, near_ids, far_ids, live, twoway):
    group = 64
    count = near_ids.shape[0]
    extra = -count % group
    near_ids = jnp.concatenate([near_ids, jnp.zeros((extra,), jnp.int32)])
    far_ids = jnp.concatenate([far_ids, jnp.zeros((extra,), jnp.int32)])
    live = jnp.concatenate([live, jnp.zeros((extra,), jnp.float32)])
    twoway = jnp.concatenate([twoway, jnp.zeros((extra,), jnp.float32)])
    turns = (count + extra) // group

    def step(total, item):
        near, far, keep, both = item
        weights = tile_weights(cent[near], cent[far]).astype(jnp.float32)
        near_u = values[near].astype(jnp.float32)
        far_u = values[far].astype(jnp.float32)
        to_near = jnp.einsum('gij,gcj->gci', weights, far_u, precision=lax.Precision.HIGHEST)
        to_far = jnp.einsum('gij,gci->gcj', weights, near_u, precision=lax.Precision.HIGHEST)
        total = total.at[near].add(to_near * keep[:, None, None])
        total = total.at[far].add(to_far * (keep * both)[:, None, None])
        return (total, None)
    start = jnp.zeros(values.shape, jnp.float32)
    items = (near_ids.reshape(turns, group), far_ids.reshape(turns, group), live.reshape(turns, group), twoway.reshape(turns, group))
    total, unused = lax.scan(step, start, items)
    return total

def reference(centroids, volumes, densities, sens_in, local_first, local_second, pair_count, pair_mine):
    parts = N_PX * N_PY
    total_blocks = parts * NB_DEV
    cent = centroids.reshape(3, total_blocks, BLK).transpose(1, 0, 2)
    weighted = jnp.stack([volumes, volumes * densities]).astype(jnp.bfloat16)
    weighted = weighted.reshape(2, total_blocks, BLK).transpose(1, 0, 2)
    own = jnp.arange(total_blocks, dtype=jnp.int32)
    owner = (jnp.arange(parts * LP, dtype=jnp.int32) // LP).astype(jnp.int32)
    local_near = owner * NB_DEV + local_first.astype(jnp.int32)
    local_far = owner * NB_DEV + local_second.astype(jnp.int32)
    upper_a, upper_b = np.triu_indices(parts, 1)
    upper_a = jnp.asarray(upper_a, dtype=jnp.int32)
    upper_b = jnp.asarray(upper_b, dtype=jnp.int32)
    cross_near = (upper_a[:, None] * NB_DEV + pair_mine[upper_a, upper_b, :]).reshape(-1).astype(jnp.int32)
    cross_far = (upper_b[:, None] * NB_DEV + pair_mine[upper_b, upper_a, :]).reshape(-1).astype(jnp.int32)
    cross_live = (jnp.arange(CAP)[None, :] < pair_count[upper_a, upper_b][:, None]).reshape(-1).astype(jnp.float32)
    near_ids = jnp.concatenate([own, local_near, cross_near])
    far_ids = jnp.concatenate([own, local_far, cross_far])
    live = jnp.concatenate([jnp.ones((total_blocks + parts * LP,), jnp.float32), cross_live])
    twoway = jnp.concatenate([jnp.zeros((total_blocks,), jnp.float32), jnp.ones((parts * LP + cross_live.shape[0],), jnp.float32)])
    totals = pair_sums(cent, weighted, near_ids, far_ids, live, twoway)
    filtered = (totals[:, 1] / totals[:, 0]).reshape(-1)
    ratio = (sens_in.reshape(total_blocks, BLK) / totals[:, 0]).astype(jnp.bfloat16)[:, None, :]
    back = pair_sums(cent, ratio, near_ids, far_ids, live, twoway)
    sensitivity = volumes * back[:, 0].reshape(-1)
    return (filtered, sensitivity)
```

```python
import functools

import jax
import jax.numpy as jnp
from jax import lax
from jax.experimental import pallas as pl
from jax.experimental.pallas import tpu as pltpu
from jax.sharding import PartitionSpec as P

BLK = 256
HALF = BLK // 2
AXES = ("px", "py")
ROWS = 8
WORDS = 5
PEER_ROWS = 24
FEATURES = 32
COORD = 16384.0
VOLUME = 21845.0
DENSITY = 65535.0
MIDDLE = 1.5
TINY = 1e-12
KEEP_LIMIT = 20 << 20
MIB = 1 << 20

VMEM = pl.BlockSpec(memory_space=pltpu.VMEM)
SMEM = pl.BlockSpec(memory_space=pltpu.SMEM)
HBM = pl.BlockSpec(memory_space=pltpu.HBM)


def fixed(value, steps):
    return (value * steps + 0.5).astype(jnp.int32)


def two_halves(first, second):
    return first | (second << 16)


def pack_kernel(chosen_in, cent_in, vol_in, dens_in, payload, words, chosen, cent, vol, dens, sems):
    blocks = words.shape[0]
    waits = fetch(
        [(cent_in, cent), (vol_in, vol), (dens_in, dens), (chosen_in, chosen)], sems
    )
    words[...] = jnp.zeros_like(words)
    for wait in waits:
        wait()
    for b in range(blocks):
        low = cent[:, b * BLK : b * BLK + HALF]
        high = cent[:, b * BLK + HALF : (b + 1) * BLK]
        words[b, 0:3, :] = two_halves(fixed(low, COORD), fixed(high, COORD))
    for row, source, steps in ((3, vol, VOLUME), (4, dens, DENSITY)):
        low = source[pl.ds(0, blocks, stride=2), :]
        high = source[pl.ds(1, blocks, stride=2), :]
        words[:, row, :] = two_halves(fixed(low, steps), fixed(high, steps))
    slots, peers = chosen.shape

    def send(p, carry):
        for s in range(slots):
            payload[p, WORDS * s : WORDS * (s + 1), :] = words[chosen[s, p], 0:WORDS, :]
        return carry

    lax.fori_loop(0, peers, send, 0, unroll=4)


def decode(word):
    row = lax.broadcasted_iota(jnp.int32, (ROWS, BLK), 0)
    step = jnp.where(
        row < 3,
        1.0 / COORD,
        jnp.where(row == 3, 1.0 / VOLUME, jnp.where(row == 4, 1.0 / DENSITY, 0.0)),
    )
    parts = jnp.concatenate([word & 0xFFFF, lax.shift_right_logical(word, 16)], axis=1)
    held = parts.astype(jnp.float32) * step
    volume = held[3:4, :]
    values = jnp.where(row == 4, held * volume, held).astype(jnp.bfloat16)
    place = jnp.where(row < 3, held - MIDDLE, 0.0)
    high = place.astype(jnp.bfloat16).astype(jnp.float32)
    low = place - high
    norm = jnp.sum(place * place, axis=0, keepdims=True)
    norm1 = norm.astype(jnp.bfloat16).astype(jnp.float32)
    rest = norm - norm1
    norm2 = rest.astype(jnp.bfloat16).astype(jnp.float32)
    norm3 = rest - norm2
    one = jnp.where(row == 6, 1.0, 0.0)
    far1 = high + jnp.where(
        row == 3, norm1, jnp.where(row == 4, norm2, jnp.where(row == 5, norm3, one))
    )
    far2 = low + jnp.where((row == 3) | (row == 4), 1.0, 0.0)
    far = jnp.concatenate([far1, far2], axis=0).astype(jnp.bfloat16)
    far = jnp.concatenate([far, far], axis=0)
    near1 = -2.0 * high + jnp.where(
        (row >= 3) & (row <= 5), 1.0, jnp.where(row == 6, norm1, 0.0)
    )
    near2 = -2.0 * high + jnp.where(row == 3, norm2, jnp.where(row == 4, norm3, 0.0))
    near34 = -2.0 * low
    near = jnp.concatenate([near1, near2, near34, near34], axis=0).astype(jnp.bfloat16)
    return far, near, values


def product(rows, tile):
    return jnp.dot(rows, tile, preferred_element_type=jnp.float32)


def product_t(rows, tile):
    return lax.dot_general(
        rows, tile, (((1,), (1,)), ((), ())), preferred_element_type=jnp.float32
    )


def cone(square):
    square = jnp.maximum(square, TINY)
    return jnp.maximum((1.0 - square * lax.rsqrt(square)).astype(jnp.bfloat16), 0)


def staged(groups, width, tiles, kept, sems, squares, square, use):
    def copy(k):
        part = pl.ds(2 * k * width, 2 * width)
        return pltpu.make_async_copy(tiles.at[part], kept.at[part], sems.at[k])

    def distances(g, slot):
        for u in range(width):
            squares[slot][u] = square(g * width + u)

    def cones(view, at, slot):
        for u in range(width):
            view[at + u] = cone(squares[slot][u])

    def sums(view, at, g):
        return [use(g * width + u, view[at + u]) for u in range(width)]

    def finish(ends):
        for end in ends:
            end()

    distances(0, 0)
    cones(tiles.at[pl.ds(0, width)], 0, 0)
    distances(1, 1)

    def turn(k, carry):
        g = 2 * k
        view = tiles.at[pl.ds((g - 2) * width, 3 * width)]
        ends = sums(view, 0, g - 2)
        cones(view, width, 1)
        distances(g, 0)
        finish(ends)
        if kept is not None:
            copy(k - 1).start()
        ends = sums(view, width, g - 1)
        cones(view, 2 * width, 0)
        distances(g + 1, 1)
        finish(ends)
        return carry

    lax.fori_loop(1, groups // 2, turn, 0)
    view = tiles.at[pl.ds((groups - 2) * width, 2 * width)]
    finish(sums(view, 0, groups - 2))
    cones(view, width, 1)
    if kept is not None:
        copy(groups // 2 - 1).start()
    finish(sums(view, width, groups - 1))

    def wait():
        def one(k, carry):
            copy(k).wait()
            return carry

        lax.fori_loop(0, groups // 2, one, 0)

    return wait


def chunked(size, width, tiles, squares, square, use):
    room = tiles.shape[0]

    def chunk(c, carry):
        base = c * room
        left = jnp.minimum(size - base, room)
        groups = even_groups(left, width)
        staged(
            groups,
            width,
            tiles,
            None,
            None,
            squares,
            lambda i: square(base + i),
            lambda i, tile: use(base + i, tile),
        )
        return carry

    lax.fori_loop(0, jnp.maximum((size + room - 1) // room, 1), chunk, 0)


def even_groups(size, width):
    return jnp.maximum((size + 2 * width - 1) // (2 * width), 1) * 2


def fetch(pairs, sems):
    copies = [pltpu.make_async_copy(a, b, sems.at[k]) for k, (a, b) in enumerate(pairs)]
    for copy in copies:
        copy.start()
    return [copy.wait for copy in copies]


def local_kernel(
    width, first_in, second_in, counts_in, words, total, kept, near, listed, size,
    first, second, counts, tiles, far_t, vals, square0, square1, sems, self_sems, pair_sems,
):
    blocks = words.shape[0]
    pairs = first.shape[0]
    peers = counts.shape[1]
    slots = listed.shape[0] // peers
    squares = (square0, square1)
    waits = fetch([(first_in, first), (second_in, second), (counts_in, counts)], sems)

    def prepare(b, carry):
        f, n, v = decode(words[b])
        far_t[b] = f.T
        near[b] = n
        vals[b] = v
        return carry

    lax.fori_loop(0, blocks, prepare, 0, unroll=4)
    for wait in waits:
        wait()

    def square_self(b):
        return product(far_t[b], near[b])

    def use_self(b, tile):
        sums = product(vals[b], tile)

        def end():
            total[b] = sums

        return end

    part = pl.ds(0, blocks)
    wait_self = staged(
        blocks // width, width, tiles.at[part], kept.at[part], self_sems, squares, square_self, use_self
    )

    def square_pair(j):
        return product(far_t[second[j]], near[first[j]])

    def use_pair(j, tile):
        a, b = first[j], second[j]
        to_first = product(vals[b], tile)
        to_second = product_t(vals[a], tile)

        def end():
            total[a] += to_first
            total[b] += to_second

        return end

    part = pl.ds(blocks, pairs)
    wait_pair = staged(
        pairs // width, width, tiles.at[part], kept.at[part], pair_sems, squares, square_pair, use_pair
    )

    def collect(p, found):
        for s in range(slots):
            listed[found] = p * slots + s
            found = found + (s < counts[0, p]).astype(jnp.int32)
        return found

    found = lax.fori_loop(0, peers, collect, 0)
    size[0] = found

    def blank(i, carry):
        listed[i] = 0
        return carry

    lax.fori_loop(found, listed.shape[0], blank, 0)
    wait_self()
    wait_pair()


def far_word(received, slots, place):
    peer, slot = place // slots, place % slots
    return received[pl.ds(peer * PEER_ROWS + slot * WORDS, ROWS), :]


def cross_kernel(
    width, keep, listed, size, chosen_in, received, near, total_in, sens_in, filtered, ratio, payload, *rest
):
    kept = None
    if keep:
        kept, *rest = rest
    tiles, total, flat, vals, sens, chosen, square0, square1, sems, *tile_sems = rest
    blocks = near.shape[0]
    waits = fetch([(chosen_in, chosen), (sens_in, sens)], sems)
    total[...] = total_in[...]
    slots, peers = chosen.shape
    ring = vals.shape[0]
    for wait in waits:
        wait()

    def mine(place):
        return chosen[place % slots, place // slots]

    def square(i):
        place = listed[i]
        f, unused, v = decode(far_word(received, slots, place))
        vals[lax.rem(i, ring)] = v
        return product(f.T, near[mine(place)])

    def use(i, tile):
        b = mine(listed[i])
        sums = product(vals[lax.rem(i, ring)], tile)
        sums = jnp.where(i < size[0], sums, 0.0)

        def end():
            total[b] += sums

        return end

    squares = (square0, square1)
    if keep:
        groups = even_groups(size[0], width)
        wait_tiles = staged(groups, width, tiles, kept, tile_sems[0], squares, square, use)
    else:
        chunked(size[0], width, tiles, squares, square, use)
    base = total[:, 3, :]
    filt = total[:, 4, :] / base
    for half in range(2):
        rows = pl.ds(half, blocks, stride=2)
        lanes = slice(half * HALF, (half + 1) * HALF)
        filtered[rows, :] = filt[:, lanes]
        part = sens[rows, :] / base[:, lanes]
        flat[rows, :] = part.astype(jnp.bfloat16).astype(jnp.float32)
    ratio[...] = jnp.zeros_like(ratio)
    for half in range(2):
        lanes = slice(half * HALF, (half + 1) * HALF)
        ratio[:, 0, lanes] = flat[pl.ds(half, blocks, stride=2), :]

    def send(p, carry):
        for s in range(slots):
            payload[p, 2 * s : 2 * s + 2, :] = flat[pl.ds(2 * chosen[s, p], 2), :]
        return carry

    lax.fori_loop(0, peers, send, 0, unroll=4)
    if keep:
        wait_tiles()


def load_groups(width, groups, kept, tiles, sems):
    def copy(k):
        part = pl.ds(k * width, width)
        return pltpu.make_async_copy(kept.at[part], tiles.at[part], sems.at[k])

    def one(k, carry):
        copy(k).start()
        return carry

    lax.fori_loop(0, groups, one, 0)
    return lambda k: copy(k).wait()


def back_local_kernel(
    width, first_in, second_in, ratio, kept, total, first, second, tiles, sems, tile_sems
):
    blocks = ratio.shape[0]
    pairs = first.shape[0]
    waits = fetch([(first_in, first), (second_in, second)], sems)
    ready = load_groups(width, (blocks + pairs) // width, kept, tiles, tile_sems)

    def rows(b):
        return ratio[b].astype(jnp.bfloat16)

    def own(k, carry):
        ready(k)
        sums = [product(rows(k * width + u), tiles[k * width + u]) for u in range(width)]
        for u in range(width):
            total[k * width + u] = sums[u]
        return carry

    lax.fori_loop(0, blocks // width, own, 0)
    for wait in waits:
        wait()

    def pair(k, carry):
        ready(blocks // width + k)
        ids = [(first[k * width + u], second[k * width + u]) for u in range(width)]
        sums = []
        for u, (a, b) in enumerate(ids):
            tile = tiles[blocks + k * width + u]
            sums.append((product(rows(b), tile), product_t(rows(a), tile)))
        for (a, b), (to_first, to_second) in zip(ids, sums):
            total[a] += to_first
            total[b] += to_second
        return carry

    lax.fori_loop(0, pairs // width, pair, 0)


def far_ratio(ratio, place):
    row0 = ratio[pl.ds(place * 2, 1), :]
    row1 = ratio[pl.ds(place * 2 + 1, 1), :]
    return jnp.concatenate([row0, row1], axis=1).astype(jnp.bfloat16)


def finish_back(blocks, vol, total, out):
    for half in range(2):
        rows = pl.ds(half, blocks, stride=2)
        lanes = slice(half * HALF, (half + 1) * HALF)
        out[rows, :] = vol[rows, :] * total[:, 0, lanes]


def back_cross_kernel(
    width, listed, size, chosen_in, ratio, kept, total_in, vol_in, out,
    total, chosen, vol, tiles, sems, tile_sems,
):
    blocks = total.shape[0]
    groups = (size[0] + width - 1) // width
    waits = fetch([(chosen_in, chosen), (vol_in, vol)], sems)
    ready = load_groups(width, groups, kept, tiles, tile_sems)
    total[...] = total_in[...]
    slots = chosen.shape[0]
    for wait in waits:
        wait()

    def turn(k, carry):
        ready(k)
        sums = []
        for u in range(width):
            i = k * width + u
            place = listed[i]
            part = product(far_ratio(ratio, place), tiles[i])
            part = jnp.where(i < size[0], part, 0.0)
            sums.append((chosen[place % slots, place // slots], part))
        for b, part in sums:
            total[b, 0:1, :] += part
        return carry

    lax.fori_loop(0, groups, turn, 0)
    finish_back(blocks, vol, total, out)


def back_again_kernel(
    width, listed, size, chosen_in, ratio, received, near, total_in, vol_in, out,
    total, chosen, vol, tiles, square0, square1, sems,
):
    blocks = total.shape[0]
    waits = fetch([(chosen_in, chosen), (vol_in, vol)], sems)
    total[...] = total_in[...]
    slots = chosen.shape[0]
    for wait in waits:
        wait()

    def mine(place):
        return chosen[place % slots, place // slots]

    def square(i):
        place = listed[i]
        f, unused, v = decode(far_word(received, slots, place))
        return product(f.T, near[mine(place)])

    def use(i, tile):
        part = jnp.where(i < size[0], product(far_ratio(ratio, listed[i]), tile), 0.0)

        def end():
            total[mine(listed[i]), 0:1, :] += part

        return end

    chunked(size[0], width, tiles, (square0, square1), square, use)
    finish_back(blocks, vol, total, out)


def in_hbm(array):
    return pltpu.with_memory_space_constraint(array, pltpu.HBM)


def params(mib):
    return pltpu.CompilerParams(vmem_limit_bytes=mib * MIB)


def shards(
    centroids, volumes, densities, sens_in, local_first, local_second, pair_count, pair_mine
):
    elements = volumes.shape[0]
    blocks = elements // BLK
    flat_rows = elements // HALF
    vol = in_hbm(volumes.reshape(flat_rows, HALF))
    dens = in_hbm(densities.reshape(flat_rows, HALF))
    sens = in_hbm(sens_in.reshape(flat_rows, HALF))
    local_first, local_second = in_hbm(local_first), in_hbm(local_second)
    chosen = in_hbm(pair_mine[0].T)
    slots, peers = chosen.shape
    places = peers * slots
    pairs = local_first.shape[0]
    f32, bf16, i32 = jnp.float32, jnp.bfloat16, jnp.int32
    shape = jax.ShapeDtypeStruct
    width = 2
    flat = pltpu.VMEM((flat_rows, HALF), f32)
    sums = pltpu.VMEM((blocks, ROWS, BLK), f32)
    square = pltpu.VMEM((width, BLK, BLK), f32)
    table = pltpu.SMEM(chosen.shape, i32)
    row = pltpu.SMEM((pairs,), i32)

    payload, words = pl.pallas_call(
        pack_kernel,
        out_shape=(shape((peers, PEER_ROWS, HALF), i32), shape((blocks, ROWS, HALF), i32)),
        in_specs=[HBM] * 4,
        out_specs=(VMEM, VMEM),
        scratch_shapes=[
            table,
            pltpu.VMEM(centroids.shape, f32),
            flat,
            flat,
            pltpu.SemaphoreType.DMA((4,)),
        ],
        compiler_params=params(8),
        name="pack",
    )(chosen, in_hbm(centroids), vol, dens)
    received = lax.all_to_all(payload, AXES, split_axis=0, concat_axis=0, tiled=True)
    total, tiles, near, listed, size = pl.pallas_call(
        functools.partial(local_kernel, width),
        out_shape=(
            shape((blocks, ROWS, BLK), f32),
            pltpu.HBM((blocks + pairs, BLK, BLK), bf16),
            shape((blocks, FEATURES, BLK), bf16),
            shape((places,), i32),
            shape((1,), i32),
        ),
        in_specs=[HBM, HBM, HBM, VMEM],
        out_specs=(VMEM, HBM, VMEM, SMEM, SMEM),
        scratch_shapes=[
            row,
            row,
            pltpu.SMEM(pair_count.shape, i32),
            pltpu.VMEM((blocks + pairs, BLK, BLK), bf16),
            pltpu.VMEM((blocks, BLK, FEATURES), bf16),
            pltpu.VMEM((blocks, ROWS, BLK), bf16),
            square,
            square,
            pltpu.SemaphoreType.DMA((3,)),
            pltpu.SemaphoreType.DMA((blocks // (2 * width),)),
            pltpu.SemaphoreType.DMA((pairs // (2 * width),)),
        ],
        compiler_params=params(48),
        cost_estimate=pl.CostEstimate(
            flops=(blocks + pairs) * BLK * BLK * 100, bytes_accessed=1 << 20, transcendentals=0
        ),
        name="local",
    )(local_first, local_second, in_hbm(pair_count), words)
    received = received.reshape(peers * PEER_ROWS, HALF)
    tile_bytes = BLK * BLK * 2
    keep = places * tile_bytes <= KEEP_LIMIT
    held = places if keep else KEEP_LIMIT // tile_bytes // (4 * width) * (4 * width)
    filtered, ratio, payload2, *cross_tiles = pl.pallas_call(
        functools.partial(cross_kernel, width, keep),
        out_shape=(
            shape((flat_rows, HALF), f32),
            shape((blocks, ROWS, BLK), f32),
            shape((peers, 2 * slots, HALF), f32),
        )
        + ((pltpu.HBM((places, BLK, BLK), bf16),) if keep else ()),
        in_specs=[SMEM, SMEM, HBM, VMEM, VMEM, VMEM, HBM],
        out_specs=(VMEM, VMEM, VMEM) + ((HBM,) if keep else ()),
        scratch_shapes=[
            pltpu.VMEM((held, BLK, BLK), bf16),
            sums,
            flat,
            pltpu.VMEM((8 * width, ROWS, BLK), bf16),
            flat,
            table,
            square,
            square,
            pltpu.SemaphoreType.DMA((2,)),
        ]
        + ([pltpu.SemaphoreType.DMA((places // (2 * width),))] if keep else []),
        compiler_params=params(48),
        name="cross",
    )(listed, size, chosen, received, near, total, sens)
    received2 = lax.all_to_all(payload2, AXES, split_axis=0, concat_axis=0, tiled=True)
    back = pl.pallas_call(
        functools.partial(back_local_kernel, 8),
        out_shape=shape((blocks, ROWS, BLK), f32),
        in_specs=[HBM, HBM, VMEM, HBM],
        out_specs=VMEM,
        scratch_shapes=[
            row,
            row,
            pltpu.VMEM((blocks + pairs, BLK, BLK), bf16),
            pltpu.SemaphoreType.DMA((2,)),
            pltpu.SemaphoreType.DMA(((blocks + pairs) // 8,)),
        ],
        compiler_params=params(48),
        cost_estimate=pl.CostEstimate(
            flops=(blocks + pairs) * BLK * BLK * 100, bytes_accessed=1 << 20, transcendentals=0
        ),
        name="back_local",
    )(local_first, local_second, ratio, in_hbm(tiles))
    received2 = received2.reshape(places * 2, HALF)
    common = [sums, table, flat, pltpu.VMEM((held, BLK, BLK), bf16)]
    if keep:
        kernel, operands, specs = back_cross_kernel, (in_hbm(cross_tiles[0]),), [HBM]
        scratch = [pltpu.SemaphoreType.DMA((2,)), pltpu.SemaphoreType.DMA((places // 8,))]
    else:
        kernel, operands, specs = back_again_kernel, (received, near), [VMEM, VMEM]
        scratch = [square, square, pltpu.SemaphoreType.DMA((2,))]
    sensitivity = pl.pallas_call(
        functools.partial(kernel, 8 if keep else width),
        out_shape=shape((flat_rows, HALF), f32),
        in_specs=[SMEM, SMEM, HBM, VMEM, *specs, VMEM, HBM],
        out_specs=VMEM,
        scratch_shapes=common + scratch,
        compiler_params=params(48),
        name="back_cross",
    )(listed, size, chosen, received2, *operands, back, vol)
    return (filtered.reshape(-1), sensitivity.reshape(-1))


def solution(mesh):
    return jax.shard_map(
        shards,
        mesh=mesh,
        in_specs=(
            P(None, AXES),
            P(AXES),
            P(AXES),
            P(AXES),
            P(AXES),
            P(AXES),
            P(AXES, None),
            P(AXES, None, None),
        ),
        out_specs=(P(AXES), P(AXES)),
        check_vma=False,
    )
```

```python
import functools

import jax
import jax.numpy as jnp
from jax import lax
from jax.experimental import pallas as pl
from jax.experimental.pallas import tpu as pltpu
from jax.sharding import PartitionSpec as P

BLK = 256
HALF = BLK // 2
AXES = ("px", "py")
ROWS = 8
WORDS = 5
PEER_ROWS = 24
FEATURES = 32
COORD = 16384.0
VOLUME = 21845.0
DENSITY = 65535.0
MIDDLE = 1.5
TINY = 4e-6
DEPTH = 6
KEEP_LIMIT = 20 << 20
MIB = 1 << 20

VMEM = pl.BlockSpec(memory_space=pltpu.VMEM)
SMEM = pl.BlockSpec(memory_space=pltpu.SMEM)
HBM = pl.BlockSpec(memory_space=pltpu.HBM)


def fixed(value, steps):
    return (value * steps + 0.5).astype(jnp.int32)


def two_halves(first, second):
    return first | (second << 16)


def pack_kernel(chosen_in, cent_in, vol_in, dens_in, payload, words, chosen, cent, vol, dens, sems):
    blocks = words.shape[0]
    waits = fetch(
        [(cent_in, cent), (vol_in, vol), (dens_in, dens), (chosen_in, chosen)], sems
    )
    words[...] = jnp.zeros_like(words)
    for wait in waits:
        wait()
    for b in range(blocks):
        low = cent[:, b * BLK : b * BLK + HALF]
        high = cent[:, b * BLK + HALF : (b + 1) * BLK]
        words[b, 0:3, :] = two_halves(fixed(low, COORD), fixed(high, COORD))
    for row, source, steps in ((3, vol, VOLUME), (4, dens, DENSITY)):
        low = source[pl.ds(0, blocks, stride=2), :]
        high = source[pl.ds(1, blocks, stride=2), :]
        words[:, row, :] = two_halves(fixed(low, steps), fixed(high, steps))
    slots, peers = chosen.shape

    def send(p, carry):
        for s in range(slots):
            payload[p, WORDS * s : WORDS * (s + 1), :] = words[chosen[s, p], 0:WORDS, :]
        return carry

    lax.fori_loop(0, peers, send, 0, unroll=4)


def decode(word):
    row = lax.broadcasted_iota(jnp.int32, (ROWS, BLK), 0)
    step = jnp.where(
        row < 3,
        1.0 / COORD,
        jnp.where(row == 3, 1.0 / VOLUME, jnp.where(row == 4, 1.0 / DENSITY, 0.0)),
    )
    parts = jnp.concatenate([word & 0xFFFF, lax.shift_right_logical(word, 16)], axis=1)
    held = parts.astype(jnp.float32) * step
    volume = held[3:4, :]
    values = jnp.where(row == 4, held * volume, held).astype(jnp.bfloat16)
    place = jnp.where(row < 3, held - MIDDLE, 0.0)
    high = place.astype(jnp.bfloat16).astype(jnp.float32)
    low = place - high
    norm = jnp.sum(place * place, axis=0, keepdims=True)
    norm1 = norm.astype(jnp.bfloat16).astype(jnp.float32)
    rest = norm - norm1
    norm2 = rest.astype(jnp.bfloat16).astype(jnp.float32)
    norm3 = rest - norm2
    one = jnp.where(row == 6, 1.0, 0.0)
    far1 = high + jnp.where(
        row == 3, norm1, jnp.where(row == 4, norm2, jnp.where(row == 5, norm3, one))
    )
    far2 = low + jnp.where((row == 3) | (row == 4), 1.0, 0.0)
    far = jnp.concatenate([far1, far2], axis=0).astype(jnp.bfloat16)
    far = jnp.concatenate([far, far], axis=0)
    near1 = -2.0 * high + jnp.where(
        (row >= 3) & (row <= 5), 1.0, jnp.where(row == 6, norm1, 0.0)
    )
    near2 = -2.0 * high + jnp.where(row == 3, norm2, jnp.where(row == 4, norm3, 0.0))
    near34 = -2.0 * low
    near = jnp.concatenate([near1, near2, near34, near34], axis=0).astype(jnp.bfloat16)
    return far, near, values


def product(rows, tile):
    return jnp.dot(rows, tile, preferred_element_type=jnp.float32)


def product_t(rows, tile):
    return lax.dot_general(
        rows, tile, (((1,), (1,)), ((), ())), preferred_element_type=jnp.float32
    )


def cone(squares, u):
    root = squares[u] * lax.rsqrt(jnp.maximum(squares[u], TINY))
    return jnp.maximum((1.0 - root).astype(jnp.bfloat16), 0)


def staged(groups, width, tiles, kept, sems, squares, results, square, use, settle, beside=None):
    def place(d, u):
        return (d % DEPTH) * width + u

    def copy(k, count):
        part = pl.ds(k * DEPTH * width, count * width)
        return pltpu.make_async_copy(tiles.at[part], kept.at[part], sems.at[k])

    def distances(g, d):
        for u in range(width):
            squares[d % 2][u] = square(g * width + u, place(d, u))

    def cones(view, d):
        for u in range(width):
            view[d * width + u] = cone(squares[d % 2], u)

    def sums(view, g, d):
        for u in range(width):
            at = place(d, u)
            for result, part in zip(results, use(g * width + u, at, view[d * width + u])):
                result[at] = part

    def settled(g, count):
        for d in range(count):
            for u in range(width):
                settle((g + d) * width + u, place(d, u))

    def view_from(g, count):
        return tiles.at[pl.ds(g * width, count * width)]

    distances(0, 0)
    distances(1, 1)
    cones(view_from(0, 1), 0)
    turns = (groups - 2) // DEPTH

    def turn(k, carry):
        g = k * DEPTH
        view = view_from(g, DEPTH + 1)
        if beside is not None:
            beside(k)
        for d in range(DEPTH):
            sums(view, g + d, d)
            distances(g + d + 2, d + 2)
            cones(view, d + 1)
        settled(g, DEPTH)
        if kept is not None:
            copy(k, DEPTH).start()
        return carry

    lax.fori_loop(0, turns, turn, 0)
    g = turns * DEPTH
    view = view_from(g, 2)
    sums(view, g, 0)
    cones(view, 1)
    if kept is not None:
        copy(turns, 2).start()
    sums(view, g + 1, 1)
    settled(g, 2)

    def wait():
        def one(k, carry):
            copy(k, DEPTH).wait()
            return carry

        lax.fori_loop(0, turns, one, 0)
        copy(turns, 2).wait()

    return wait


def padded(groups):
    return jnp.maximum((groups - 2 + DEPTH - 1) // DEPTH, 0) * DEPTH + 2


def chunked(size, room, width, ring, squares, results, square, use, settle):
    def chunk(c, carry):
        base = c * room
        left = jnp.minimum(size - base, room)
        staged(
            padded((left + width - 1) // width),
            width,
            ring,
            None,
            None,
            squares,
            results,
            lambda i, at: square(base + i, at),
            lambda i, at, tile: use(base + i, at, tile),
            lambda i, at: settle(jnp.where(i < left, base + i, size), at),
        )
        return carry

    lax.fori_loop(0, jnp.maximum((size + room - 1) // room, 1), chunk, 0)


def fetch(pairs, sems):
    copies = [pltpu.make_async_copy(a, b, sems.at[k]) for k, (a, b) in enumerate(pairs)]
    for copy in copies:
        copy.start()
    return [copy.wait for copy in copies]


def local_kernel(
    width, first_in, second_in, counts_in, chosen_in, words, total, kept, near, plan,
    first, second, counts, chosen, ring, far_t, vals, square0, square1, sums0, sums1, sems, self_sems, pair_sems,
):
    blocks = words.shape[0]
    pairs = first.shape[0]
    peers = counts.shape[1]
    squares = (square0, square1)
    slots = chosen.shape[0]
    waits = fetch(
        [(first_in, first), (second_in, second), (counts_in, counts), (chosen_in, chosen)], sems
    )

    def prepare(b, carry):
        f, n, v = decode(words[b])
        far_t[b] = f.T
        near[b] = n
        vals[b] = v
        return carry

    lax.fori_loop(0, blocks, prepare, 0, unroll=8)
    for wait in waits:
        wait()

    def square_self(b, at):
        return product(far_t[b], near[b])

    def use_self(b, at, tile):
        return (product(vals[b], tile),)

    def settle_self(b, at):
        total[b] = sums0[at]

    length = plan_length(plan)
    turns = (blocks // width - 2) // DEPTH
    share = -(-peers // turns)
    plan[0] = 0

    def collect(k):
        found = plan[0]
        for q in range(share):
            p = k * share + q
            peer = jnp.minimum(p, peers - 1)
            count = jnp.where(p < peers, counts[0, peer], 0)
            for s in range(slots):
                plan[1 + found] = peer * slots + s
                plan[1 + length + found] = chosen[s, peer]
                found = found + (s < count).astype(jnp.int32)
        plan[0] = found

    part = pl.ds(0, blocks)
    wait_self = staged(
        blocks // width, width, ring.at[part], kept.at[part], self_sems, squares, (sums0,),
        square_self, use_self, settle_self, collect,
    )

    def square_pair(j, at):
        return product(far_t[second[j]], near[first[j]])

    def use_pair(j, at, tile):
        return product(vals[second[j]], tile), product_t(vals[first[j]], tile)

    def settle_pair(j, at):
        total[first[j]] += sums0[at]
        total[second[j]] += sums1[at]

    part = pl.ds(blocks, pairs)
    wait_pair = staged(
        pairs // width, width, ring.at[part], kept.at[part], pair_sems, squares, (sums0, sums1),
        square_pair, use_pair, settle_pair,
    )

    for i in range(2 * DEPTH * width):
        plan[1 + plan[0] + i] = 0
        plan[1 + length + plan[0] + i] = 0
    wait_self()
    wait_pair()


def plan_length(plan):
    return (plan.shape[0] - 1) // 2


def far_word(received, slots, place):
    peer, slot = place // slots, place % slots
    return received[pl.ds(peer * PEER_ROWS + slot * WORDS, ROWS), :]


def cross_kernel(
    width, keep, plan, chosen_in, received, near, total_in, sens_in, filtered, ratio, payload, *rest
):
    kept = None
    if keep:
        kept, *rest = rest
    ring, total, flat, vals, sens, chosen, square0, square1, sums0, sems, *ring_sems = rest
    blocks = near.shape[0]
    waits = fetch([(chosen_in, chosen), (sens_in, sens)], sems)
    total[...] = total_in[...]
    slots, peers = chosen.shape
    size, length = plan[0], plan_length(plan)

    def square(i, at):
        f, unused, v = decode(far_word(received, slots, plan[1 + i]))
        vals[at] = v
        return product(f.T, near[plan[1 + length + i]])

    def use(i, at, tile):
        return (product(vals[at], tile),)

    def settle(i, at):
        total[plan[1 + length + i]] += jnp.where(i < size, sums0[at], 0.0)

    squares = (square0, square1)
    if keep:
        groups = padded((size + width - 1) // width)
        wait_tiles = staged(
            groups, width, ring, kept, ring_sems[0], squares, (sums0,), square, use, settle
        )
    else:
        room = ring.shape[0] - (DEPTH + 2) * width
        chunked(size, room, width, ring, squares, (sums0,), square, use, settle)
    for wait in waits:
        wait()
    base = total[:, 3, :]
    filt = total[:, 4, :] / base
    for half in range(2):
        rows = pl.ds(half, blocks, stride=2)
        lanes = slice(half * HALF, (half + 1) * HALF)
        filtered[rows, :] = filt[:, lanes]
        part = sens[rows, :] / base[:, lanes]
        flat[rows, :] = part.astype(jnp.bfloat16).astype(jnp.float32)
    ratio[...] = jnp.zeros_like(ratio)
    for half in range(2):
        lanes = slice(half * HALF, (half + 1) * HALF)
        ratio[:, 0, lanes] = flat[pl.ds(half, blocks, stride=2), :]

    def send(p, carry):
        for s in range(slots):
            payload[p, 2 * s : 2 * s + 2, :] = flat[pl.ds(2 * chosen[s, p], 2), :]
        return carry

    lax.fori_loop(0, peers, send, 0, unroll=4)
    if keep:
        wait_tiles()


def load_groups(width, groups, kept, tiles, sems):
    def copy(k):
        part = pl.ds(k * width, width)
        return pltpu.make_async_copy(kept.at[part], tiles.at[part], sems.at[k])

    def one(k, carry):
        copy(k).start()
        return carry

    lax.fori_loop(0, groups, one, 0)
    return lambda k: copy(k).wait()


def back_local_kernel(
    width, first_in, second_in, ratio, kept, total, first, second, tiles, sems, tile_sems
):
    blocks = ratio.shape[0]
    pairs = first.shape[0]
    waits = fetch([(first_in, first), (second_in, second)], sems)
    ready = load_groups(width, (blocks + pairs) // width, kept, tiles, tile_sems)

    def rows(b):
        return ratio[b].astype(jnp.bfloat16)

    def own(k, carry):
        ready(k)
        sums = [product(rows(k * width + u), tiles[k * width + u]) for u in range(width)]
        for u in range(width):
            total[k * width + u] = sums[u]
        return carry

    lax.fori_loop(0, blocks // width, own, 0)
    for wait in waits:
        wait()

    def pair(k, carry):
        ready(blocks // width + k)
        ids = [(first[k * width + u], second[k * width + u]) for u in range(width)]
        sums = []
        for u, (a, b) in enumerate(ids):
            tile = tiles[blocks + k * width + u]
            sums.append((product(rows(b), tile), product_t(rows(a), tile)))
        for (a, b), (to_first, to_second) in zip(ids, sums):
            total[a] += to_first
            total[b] += to_second
        return carry

    lax.fori_loop(0, pairs // width, pair, 0)


def far_ratio(ratio, place):
    row0 = ratio[pl.ds(place * 2, 1), :]
    row1 = ratio[pl.ds(place * 2 + 1, 1), :]
    return jnp.concatenate([row0, row1], axis=1).astype(jnp.bfloat16)


def finish_back(blocks, vol, total, out):
    for half in range(2):
        rows = pl.ds(half, blocks, stride=2)
        lanes = slice(half * HALF, (half + 1) * HALF)
        out[rows, :] = vol[rows, :] * total[:, 0, lanes]


def back_cross_kernel(
    width, plan, ratio, kept, total_in, vol_in, out, total, vol, tiles, sems, tile_sems,
):
    blocks = total.shape[0]
    size, length = plan[0], plan_length(plan)
    groups = (size + width - 1) // width
    ready = load_groups(width, groups, kept, tiles, tile_sems)
    waits = fetch([(vol_in, vol)], sems)
    total[...] = total_in[...]

    def turn(k, carry):
        ready(k)
        sums = []
        for u in range(width):
            i = k * width + u
            part = product(far_ratio(ratio, plan[1 + i]), tiles[i])
            part = jnp.where(i < size, part, 0.0)
            sums.append((plan[1 + length + i], part))
        for b, part in sums:
            total[b, 0:1, :] += part
        return carry

    lax.fori_loop(0, groups, turn, 0)
    for wait in waits:
        wait()
    finish_back(blocks, vol, total, out)


def back_again_kernel(
    width, slots, plan, ratio, received, near, total_in, vol_in, out,
    total, vol, ring, square0, square1, sums0, sems,
):
    blocks = total.shape[0]
    waits = fetch([(vol_in, vol)], sems)
    total[...] = total_in[...]
    size, length = plan[0], plan_length(plan)

    def square(i, at):
        f, unused, v = decode(far_word(received, slots, plan[1 + i]))
        return product(f.T, near[plan[1 + length + i]])

    def use(i, at, tile):
        return (product(far_ratio(ratio, plan[1 + i]), tile),)

    def settle(i, at):
        total[plan[1 + length + i], 0:1, :] += jnp.where(i < size, sums0[at], 0.0)

    room = ring.shape[0] - (DEPTH + 2) * width
    chunked(size, room, width, ring, (square0, square1), (sums0,), square, use, settle)
    for wait in waits:
        wait()
    finish_back(blocks, vol, total, out)


def in_hbm(array):
    return pltpu.with_memory_space_constraint(array, pltpu.HBM)


def params(mib):
    return pltpu.CompilerParams(vmem_limit_bytes=mib * MIB)


def shards(
    centroids, volumes, densities, sens_in, local_first, local_second, pair_count, pair_mine
):
    elements = volumes.shape[0]
    blocks = elements // BLK
    flat_rows = elements // HALF
    vol = in_hbm(volumes.reshape(flat_rows, HALF))
    dens = in_hbm(densities.reshape(flat_rows, HALF))
    sens = in_hbm(sens_in.reshape(flat_rows, HALF))
    local_first, local_second = in_hbm(local_first), in_hbm(local_second)
    chosen = in_hbm(pair_mine[0].T)
    slots, peers = chosen.shape
    places = peers * slots
    pairs = local_first.shape[0]
    longest = 2 * places
    f32, bf16, i32 = jnp.float32, jnp.bfloat16, jnp.int32
    shape = jax.ShapeDtypeStruct
    width = 2
    flat = pltpu.VMEM((flat_rows, HALF), f32)
    sums = pltpu.VMEM((blocks, ROWS, BLK), f32)
    square = pltpu.VMEM((width, BLK, BLK), f32)
    tile_bytes = BLK * BLK * 2
    keep = places * tile_bytes <= KEEP_LIMIT
    turns = -(-(places // width - 2) // DEPTH)
    held = (turns * DEPTH + 2) * width
    ring = pltpu.VMEM((held if keep else KEEP_LIMIT // tile_bytes, BLK, BLK), bf16)
    results = pltpu.VMEM((DEPTH * width, ROWS, BLK), f32)
    ring_sems = pltpu.SemaphoreType.DMA((turns + 1,))
    table = pltpu.SMEM(chosen.shape, i32)
    row = pltpu.SMEM((pairs,), i32)

    payload, words = pl.pallas_call(
        pack_kernel,
        out_shape=(shape((peers, PEER_ROWS, HALF), i32), shape((blocks, ROWS, HALF), i32)),
        in_specs=[HBM] * 4,
        out_specs=(VMEM, VMEM),
        scratch_shapes=[
            table,
            pltpu.VMEM(centroids.shape, f32),
            flat,
            flat,
            pltpu.SemaphoreType.DMA((4,)),
        ],
        compiler_params=params(8),
        name="pack",
    )(chosen, in_hbm(centroids), vol, dens)
    received = lax.all_to_all(payload, AXES, split_axis=0, concat_axis=0, tiled=True)
    total, tiles, near, plan = pl.pallas_call(
        functools.partial(local_kernel, width),
        out_shape=(
            shape((blocks, ROWS, BLK), f32),
            pltpu.HBM((blocks + pairs, BLK, BLK), bf16),
            shape((blocks, FEATURES, BLK), bf16),
            shape((1 + 2 * longest,), i32),
        ),
        in_specs=[HBM, HBM, HBM, HBM, VMEM],
        out_specs=(VMEM, HBM, VMEM, SMEM),
        scratch_shapes=[
            row,
            row,
            pltpu.SMEM(pair_count.shape, i32),
            table,
            pltpu.VMEM((blocks + pairs, BLK, BLK), bf16),
            pltpu.VMEM((blocks, BLK, FEATURES), bf16),
            pltpu.VMEM((blocks, ROWS, BLK), bf16),
            square,
            square,
            results,
            results,
            pltpu.SemaphoreType.DMA((4,)),
            pltpu.SemaphoreType.DMA((blocks // width // DEPTH + 1,)),
            pltpu.SemaphoreType.DMA((pairs // width // DEPTH + 1,)),
        ],
        compiler_params=params(48),
        cost_estimate=pl.CostEstimate(
            flops=(blocks + pairs) * BLK * BLK * 100, bytes_accessed=1 << 20, transcendentals=0
        ),
        name="local",
    )(local_first, local_second, in_hbm(pair_count), chosen, words)
    received = received.reshape(peers * PEER_ROWS, HALF)
    filtered, ratio, payload2, *cross_tiles = pl.pallas_call(
        functools.partial(cross_kernel, width, keep),
        out_shape=(
            shape((flat_rows, HALF), f32),
            shape((blocks, ROWS, BLK), f32),
            shape((peers, 2 * slots, HALF), f32),
        )
        + ((pltpu.HBM((held, BLK, BLK), bf16),) if keep else ()),
        in_specs=[SMEM, HBM, VMEM, VMEM, VMEM, HBM],
        out_specs=(VMEM, VMEM, VMEM) + ((HBM,) if keep else ()),
        scratch_shapes=[
            ring,
            sums,
            flat,
            pltpu.VMEM((DEPTH * width, ROWS, BLK), bf16),
            flat,
            table,
            square,
            square,
            results,
            pltpu.SemaphoreType.DMA((2,)),
        ]
        + ([ring_sems] if keep else []),
        compiler_params=params(48),
        name="cross",
    )(plan, chosen, received, near, total, sens)
    received2 = lax.all_to_all(payload2, AXES, split_axis=0, concat_axis=0, tiled=True)
    back = pl.pallas_call(
        functools.partial(back_local_kernel, 8),
        out_shape=shape((blocks, ROWS, BLK), f32),
        in_specs=[HBM, HBM, VMEM, HBM],
        out_specs=VMEM,
        scratch_shapes=[
            row,
            row,
            pltpu.VMEM((blocks + pairs, BLK, BLK), bf16),
            pltpu.SemaphoreType.DMA((2,)),
            pltpu.SemaphoreType.DMA(((blocks + pairs) // 8,)),
        ],
        compiler_params=params(48),
        cost_estimate=pl.CostEstimate(
            flops=(blocks + pairs) * BLK * BLK * 100, bytes_accessed=1 << 20, transcendentals=0
        ),
        name="back_local",
    )(local_first, local_second, ratio, in_hbm(tiles))
    received2 = received2.reshape(places * 2, HALF)
    common = [sums, flat, pltpu.VMEM((places, BLK, BLK), bf16) if keep else ring]
    if keep:
        kernel, operands, specs = back_cross_kernel, (in_hbm(cross_tiles[0]),), [HBM]
        kernel = functools.partial(kernel, 8)
        scratch = [pltpu.SemaphoreType.DMA((1,)), pltpu.SemaphoreType.DMA((places // 8,))]
    else:
        kernel, operands, specs = back_again_kernel, (received, near), [VMEM, VMEM]
        scratch = [square, square, pltpu.VMEM((DEPTH * width, 1, BLK), f32), pltpu.SemaphoreType.DMA((1,))]
        kernel = functools.partial(kernel, width, slots)
    sensitivity = pl.pallas_call(
        kernel,
        out_shape=shape((flat_rows, HALF), f32),
        in_specs=[SMEM, VMEM, *specs, VMEM, HBM],
        out_specs=VMEM,
        scratch_shapes=common + scratch,
        compiler_params=params(48),
        name="back_cross",
    )(plan, received2, *operands, back, vol)
    return (filtered.reshape(-1), sensitivity.reshape(-1))


def solution(mesh):
    return jax.shard_map(
        shards,
        mesh=mesh,
        in_specs=(
            P(None, AXES),
            P(AXES),
            P(AXES),
            P(AXES),
            P(AXES),
            P(AXES),
            P(AXES, None),
            P(AXES, None, None),
        ),
        out_specs=(P(AXES), P(AXES)),
        check_vma=False,
    )
```

```python
import functools

import jax
import jax.numpy as jnp
from jax import lax
from jax.experimental import pallas as pl
from jax.experimental.pallas import tpu as pltpu
from jax.sharding import PartitionSpec as P

BLK = 256
HALF = BLK // 2
AXES = ("px", "py")
ROWS = 8
WORDS = 5
PEER_ROWS = 24
FEATURES = 32
COORD = 16384.0
VOLUME = 21845.0
DENSITY = 65535.0
MIDDLE = 1.5
TINY = 4e-6
BACK = 16
LOAD = 4
WIDTH = 1
LOOK = 3
DEPTH = 12
KEEP_LIMIT = 20 << 20
MIB = 1 << 20

VMEM = pl.BlockSpec(memory_space=pltpu.VMEM)
SMEM = pl.BlockSpec(memory_space=pltpu.SMEM)
HBM = pl.BlockSpec(memory_space=pltpu.HBM)


def fixed(value, steps):
    return (value * steps + 0.5).astype(jnp.int32)


def two_halves(first, second):
    return first | (second << 16)


def pack_kernel(chosen_in, cent_in, vol_in, dens_in, payload, words, chosen, cent, vol, dens, sems):
    blocks = words.shape[0]
    waits = fetch(
        [(cent_in, cent), (vol_in, vol), (dens_in, dens), (chosen_in, chosen)], sems
    )
    words[...] = jnp.zeros_like(words)
    for wait in waits:
        wait()
    for b in range(blocks):
        low = cent[:, b * BLK : b * BLK + HALF]
        high = cent[:, b * BLK + HALF : (b + 1) * BLK]
        words[b, 0:3, :] = two_halves(fixed(low, COORD), fixed(high, COORD))
    for row, source, steps in ((3, vol, VOLUME), (4, dens, DENSITY)):
        low = source[pl.ds(0, blocks, stride=2), :]
        high = source[pl.ds(1, blocks, stride=2), :]
        words[:, row, :] = two_halves(fixed(low, steps), fixed(high, steps))
    slots, peers = chosen.shape

    def send(p, carry):
        for s in range(slots):
            payload[p, WORDS * s : WORDS * (s + 1), :] = words[chosen[s, p], 0:WORDS, :]
        return carry

    lax.fori_loop(0, peers, send, 0, unroll=4)


def decode(word):
    row = lax.broadcasted_iota(jnp.int32, (ROWS, BLK), 0)
    step = jnp.where(
        row < 3,
        1.0 / COORD,
        jnp.where(row == 3, 1.0 / VOLUME, jnp.where(row == 4, 1.0 / DENSITY, 0.0)),
    )
    parts = jnp.concatenate([word & 0xFFFF, lax.shift_right_logical(word, 16)], axis=1)
    held = parts.astype(jnp.float32) * step
    volume = held[3:4, :]
    values = jnp.where(row == 4, held * volume, held).astype(jnp.bfloat16)
    place = jnp.where(row < 3, held - MIDDLE, 0.0)
    high = place.astype(jnp.bfloat16).astype(jnp.float32)
    low = place - high
    norm = jnp.sum(place * place, axis=0, keepdims=True)
    norm1 = norm.astype(jnp.bfloat16).astype(jnp.float32)
    rest = norm - norm1
    norm2 = rest.astype(jnp.bfloat16).astype(jnp.float32)
    norm3 = rest - norm2
    one = jnp.where(row == 6, 1.0, 0.0)
    far1 = high + jnp.where(
        row == 3, norm1, jnp.where(row == 4, norm2, jnp.where(row == 5, norm3, one))
    )
    far2 = low + jnp.where((row == 3) | (row == 4), 1.0, 0.0)
    far = jnp.concatenate([far1, far2], axis=0).astype(jnp.bfloat16)
    far = jnp.concatenate([far, far], axis=0)
    near1 = -2.0 * high + jnp.where(
        (row >= 3) & (row <= 5), 1.0, jnp.where(row == 6, norm1, 0.0)
    )
    near2 = -2.0 * high + jnp.where(row == 3, norm2, jnp.where(row == 4, norm3, 0.0))
    near34 = -2.0 * low
    near = jnp.concatenate([near1, near2, near34, near34], axis=0).astype(jnp.bfloat16)
    return far, near, values


def product(rows, tile):
    return jnp.dot(rows, tile, preferred_element_type=jnp.float32)


def product_t(rows, tile):
    return lax.dot_general(
        rows, tile, (((1,), (1,)), ((), ())), preferred_element_type=jnp.float32
    )


def cone(squares, u):
    root = squares[u] * lax.rsqrt(jnp.maximum(squares[u], TINY))
    return jnp.maximum((1.0 - root).astype(jnp.bfloat16), 0)


def staged(groups, peel, width, tiles, kept, sems, squares, results, square, use, settle, beside=None):
    def place(d, u):
        return d % DEPTH * width + u

    def copy(k, count):
        part = pl.ds(k * DEPTH * width, count * width)
        return pltpu.make_async_copy(tiles.at[part], kept.at[part], sems.at[k])

    slots = LOOK + 1

    def distances(g, d):
        for u in range(width):
            squares[(d % slots) * width + u] = square(g * width + u, place(d, u))

    def cones(view, d):
        for u in range(width):
            view[d * width + u] = cone(squares, (d % slots) * width + u)

    def sums(view, g, d):
        for u in range(width):
            parts = use(g * width + u, place(d, u), view[d * width + u])
            for result, part in zip(results, parts):
                result[d * width + u] = part

    def settled(g, count):
        for d in range(count):
            for u in range(width):
                settle((g + d) * width + u, d * width + u)

    def view_from(g, count):
        return tiles.at[pl.ds(g * width, count * width)]

    for d in range(slots):
        distances(d, d)
    cones(view_from(0, 1), 0)
    turns = (groups - slots - peel) // DEPTH

    def steps(g, count):
        view = view_from(g, count + 1)
        for d in range(count):
            sums(view, g + d, d)
            distances(g + d + slots, d + slots)
            cones(view, d + 1)
        settled(g, count)

    def turn(k, carry):
        if beside is not None:
            beside(k)
        steps(k * DEPTH, DEPTH)
        if kept is not None:
            copy(k, DEPTH).start()
        return carry

    lax.fori_loop(0, turns, turn, 0)
    g = turns * DEPTH
    last = peel + slots
    view = view_from(g, last)
    for d in range(last):
        sums(view, g + d, d)
        if d < peel:
            distances(g + d + slots, d + slots)
        if d + 1 < last:
            cones(view, d + 1)
    if kept is not None:
        copy(turns, last).start()
    settled(g, last)

    def wait():
        def one(k, carry):
            copy(k, DEPTH).wait()
            return carry

        lax.fori_loop(0, turns, one, 0)
        copy(turns, last).wait()

    return wait


def peeled(most):
    return (most - LOOK - 1) % DEPTH


def padded(groups, peel):
    least = LOOK + 1 + peel
    return jnp.maximum((groups - least + DEPTH - 1) // DEPTH, 0) * DEPTH + least


def chunked(size, room, width, ring, squares, results, square, use, settle):
    def chunk(c, carry):
        base = c * room
        left = jnp.minimum(size - base, room)
        staged(
            padded((left + width - 1) // width, 0),
            0,
            width,
            ring,
            None,
            None,
            squares,
            results,
            lambda i, at: square(base + i, at),
            lambda i, at, tile: use(base + i, at, tile),
            lambda i, at: settle(jnp.where(i < left, base + i, size), at),
        )
        return carry

    lax.fori_loop(0, jnp.maximum((size + room - 1) // room, 1), chunk, 0)


def fetch(pairs, sems):
    copies = [pltpu.make_async_copy(a, b, sems.at[k]) for k, (a, b) in enumerate(pairs)]
    for copy in copies:
        copy.start()
    return [copy.wait for copy in copies]


def local_kernel(
    width, first_in, second_in, counts_in, chosen_in, words, total, kept, near, plan,
    first, second, counts, chosen, ring, far_t, vals, squares, sums0, sums1, sems, self_sems, pair_sems,
):
    blocks = words.shape[0]
    pairs = first.shape[0]
    peers = counts.shape[1]
    slots = chosen.shape[0]
    waits = fetch(
        [(first_in, first), (second_in, second), (counts_in, counts), (chosen_in, chosen)], sems
    )

    def square_self(b, at):
        f, n, v = decode(words[b])
        f = f.T
        far_t[b] = f
        near[b] = n
        vals[b] = v
        return product(f, n)

    def use_self(b, at, tile):
        return (product(vals[b], tile),)

    def settle_self(b, at):
        total[b] = sums0[at]

    part = pl.ds(0, blocks)
    wait_self = staged(
        blocks // width, peeled(blocks // width), width, ring.at[part], kept.at[part], self_sems, squares, (sums0,),
        square_self, use_self, settle_self,
    )
    for wait in waits:
        wait()

    def square_pair(j, at):
        return product(far_t[second[j]], near[first[j]])

    def use_pair(j, at, tile):
        return product(vals[second[j]], tile), product_t(vals[first[j]], tile)

    def settle_pair(j, at):
        total[first[j]] += sums0[at]
        total[second[j]] += sums1[at]

    length = plan_length(plan)
    turns = (pairs // width - LOOK - 1) // DEPTH
    share = -(-peers // turns)
    plan[0] = 0

    def collect(k):
        found = plan[0]
        for q in range(share):
            p = k * share + q
            peer = jnp.minimum(p, peers - 1)
            count = jnp.where(p < peers, counts[0, peer], 0)
            for s in range(slots):
                plan[1 + found] = peer * slots + s
                plan[1 + length + found] = chosen[s, peer]
                found = found + (s < count).astype(jnp.int32)
        plan[0] = found

    part = pl.ds(blocks, pairs)
    wait_pair = staged(
        pairs // width, peeled(pairs // width), width, ring.at[part], kept.at[part], pair_sems, squares, (sums0, sums1),
        square_pair, use_pair, settle_pair, collect,
    )

    for i in range(2 * DEPTH * width):
        plan[1 + plan[0] + i] = 0
        plan[1 + length + plan[0] + i] = 0
    wait_self()
    wait_pair()


def plan_length(plan):
    return (plan.shape[0] - 1) // 2


def far_word(received, slots, place):
    peer, slot = place // slots, place % slots
    return received[pl.ds(peer * PEER_ROWS + slot * WORDS, ROWS), :]


def cross_kernel(
    width, keep, plan, chosen_in, received, near, total_in, sens_in, filtered, ratio, payload, *rest
):
    kept = None
    if keep:
        kept, *rest = rest
    ring, total, flat, vals, sens, chosen, squares, sums0, sems, *ring_sems = rest
    blocks = near.shape[0]
    waits = fetch([(chosen_in, chosen), (sens_in, sens)], sems)
    total[...] = total_in[...]
    slots, peers = chosen.shape
    size, length = plan[0], plan_length(plan)

    def square(i, at):
        f, unused, v = decode(far_word(received, slots, plan[1 + i]))
        vals[at] = v
        return product(f.T, near[plan[1 + length + i]])

    def use(i, at, tile):
        return (product(vals[at], tile),)

    def settle(i, at):
        total[plan[1 + length + i]] += jnp.where(i < size, sums0[at], 0.0)

    if keep:
        peel = peeled((peers - 1) * slots // width)
        groups = padded((size + width - 1) // width, peel)
        wait_tiles = staged(
            groups, peel, width, ring, kept, ring_sems[0], squares, (sums0,), square, use, settle
        )
    else:
        room = ring.shape[0] - (DEPTH + LOOK + 1) * width
        chunked(size, room, width, ring, squares, (sums0,), square, use, settle)
    for wait in waits:
        wait()
    base = total[:, 3, :]
    filt = total[:, 4, :] / base
    for half in range(2):
        rows = pl.ds(half, blocks, stride=2)
        lanes = slice(half * HALF, (half + 1) * HALF)
        filtered[rows, :] = filt[:, lanes]
        part = sens[rows, :] / base[:, lanes]
        flat[rows, :] = part.astype(jnp.bfloat16).astype(jnp.float32)
    ratio[...] = jnp.zeros_like(ratio)
    for half in range(2):
        lanes = slice(half * HALF, (half + 1) * HALF)
        ratio[:, 0, lanes] = flat[pl.ds(half, blocks, stride=2), :]

    def send(p, carry):
        for s in range(slots):
            payload[p, 2 * s : 2 * s + 2, :] = flat[pl.ds(2 * chosen[s, p], 2), :]
        return carry

    lax.fori_loop(0, peers, send, 0, unroll=4)
    if keep:
        wait_tiles()


def tile_loads(width, kept, tiles, sems):
    each = width // LOAD

    def copy(k):
        part = pl.ds(k * LOAD, LOAD)
        return pltpu.make_async_copy(kept.at[part], tiles.at[part], sems.at[k])

    def start(a, b):
        def one(k, carry):
            copy(k).start()
            return carry

        lax.fori_loop(a * each, b * each, one, 0)

    def ready(k):
        for j in range(each):
            copy(k * each + j).wait()

    return start, ready


def back_local_kernel(
    width, first_in, second_in, ratio, kept, total, first, second, tiles, sems, tile_sems
):
    blocks = ratio.shape[0]
    pairs = first.shape[0]
    start, ready = tile_loads(width, kept, tiles, tile_sems)
    waits = fetch([(first_in, first), (second_in, second)], sems)
    start(blocks // width, (blocks + pairs) // width)
    start(0, blocks // width)
    total[...] = jnp.zeros_like(total)

    def rows(b):
        return ratio[b].astype(jnp.bfloat16)

    for wait in waits:
        wait()

    def pair(k, carry):
        ready(blocks // width + k)
        ids = [(first[k * width + u], second[k * width + u]) for u in range(width)]
        sums = []
        for u, (a, b) in enumerate(ids):
            tile = tiles[blocks + k * width + u]
            sums.append((product(rows(b), tile), product_t(rows(a), tile)))
        for (a, b), (to_first, to_second) in zip(ids, sums):
            total[a] += to_first
            total[b] += to_second
        return carry

    lax.fori_loop(0, pairs // width, pair, 0)

    def own(k, carry):
        ready(k)
        sums = [product(rows(k * width + u), tiles[k * width + u]) for u in range(width)]
        for u in range(width):
            total[k * width + u] += sums[u]
        return carry

    lax.fori_loop(0, blocks // width, own, 0)


def far_ratio(ratio, place):
    row0 = ratio[pl.ds(place * 2, 1), :]
    row1 = ratio[pl.ds(place * 2 + 1, 1), :]
    return jnp.concatenate([row0, row1], axis=1).astype(jnp.bfloat16)


def finish_back(blocks, vol, total, out):
    for half in range(2):
        rows = pl.ds(half, blocks, stride=2)
        lanes = slice(half * HALF, (half + 1) * HALF)
        out[rows, :] = vol[rows, :] * total[:, 0, lanes]


def back_cross_kernel(
    width, least, plan_in, ratio, kept, total_in, vol_in, out,
    total, vol, tiles, plan, sems, tile_sems,
):
    blocks = total.shape[0]
    start, ready = tile_loads(width, kept, tiles, tile_sems)
    wait_plan, *waits = fetch([(plan_in, plan), (vol_in, vol)], sems)
    early = -(-least // width)
    start(0, early)
    total[...] = total_in[...]
    wait_plan()
    size, length = plan[0], plan_length(plan)
    groups = (size + width - 1) // width
    start(early, groups)

    def turn(k, carry):
        ready(k)
        sums = []
        for u in range(width):
            i = k * width + u
            part = product(far_ratio(ratio, plan[1 + i]), tiles[i])
            part = jnp.where(i < size, part, 0.0)
            sums.append((plan[1 + length + i], part))
        for b, part in sums:
            total[b, 0:1, :] += part
        return carry

    lax.fori_loop(0, groups, turn, 0)
    for wait in waits:
        wait()
    finish_back(blocks, vol, total, out)


def back_again_kernel(
    width, slots, plan, ratio, received, near, total_in, vol_in, out,
    total, vol, ring, squares, sums0, sems,
):
    blocks = total.shape[0]
    waits = fetch([(vol_in, vol)], sems)
    total[...] = total_in[...]
    size, length = plan[0], plan_length(plan)

    def square(i, at):
        f, unused, v = decode(far_word(received, slots, plan[1 + i]))
        return product(f.T, near[plan[1 + length + i]])

    def use(i, at, tile):
        return (product(far_ratio(ratio, plan[1 + i]), tile),)

    def settle(i, at):
        total[plan[1 + length + i], 0:1, :] += jnp.where(i < size, sums0[at], 0.0)

    room = ring.shape[0] - (DEPTH + LOOK + 1) * width
    chunked(size, room, width, ring, squares, (sums0,), square, use, settle)
    for wait in waits:
        wait()
    finish_back(blocks, vol, total, out)


def in_hbm(array):
    return pltpu.with_memory_space_constraint(array, pltpu.HBM)


def params(mib):
    return pltpu.CompilerParams(vmem_limit_bytes=mib * MIB)


def shards(
    centroids, volumes, densities, sens_in, local_first, local_second, pair_count, pair_mine
):
    elements = volumes.shape[0]
    blocks = elements // BLK
    flat_rows = elements // HALF
    vol = in_hbm(volumes.reshape(flat_rows, HALF))
    dens = in_hbm(densities.reshape(flat_rows, HALF))
    sens = in_hbm(sens_in.reshape(flat_rows, HALF))
    local_first, local_second = in_hbm(local_first), in_hbm(local_second)
    chosen = in_hbm(pair_mine[0].T)
    slots, peers = chosen.shape
    places = peers * slots
    pairs = local_first.shape[0]
    longest = 2 * places
    f32, bf16, i32 = jnp.float32, jnp.bfloat16, jnp.int32
    shape = jax.ShapeDtypeStruct
    width = WIDTH
    flat = pltpu.VMEM((flat_rows, HALF), f32)
    sums = pltpu.VMEM((blocks, ROWS, BLK), f32)
    square = pltpu.VMEM(((LOOK + 1) * width, BLK, BLK), f32)
    tile_bytes = BLK * BLK * 2
    keep = places * tile_bytes <= KEEP_LIMIT
    most = (places - slots) // width
    turns = most // DEPTH
    held = max(most * width, -(-most * width // BACK) * BACK)
    ring = pltpu.VMEM((held if keep else KEEP_LIMIT // tile_bytes, BLK, BLK), bf16)
    steps = DEPTH + LOOK + 1
    results = pltpu.VMEM((steps * width, ROWS, BLK), f32)
    ring_sems = pltpu.SemaphoreType.DMA((turns + 1,))
    table = pltpu.SMEM(chosen.shape, i32)
    row = pltpu.SMEM((pairs,), i32)

    payload, words = pl.pallas_call(
        pack_kernel,
        out_shape=(shape((peers, PEER_ROWS, HALF), i32), shape((blocks, ROWS, HALF), i32)),
        in_specs=[HBM] * 4,
        out_specs=(VMEM, VMEM),
        scratch_shapes=[
            table,
            pltpu.VMEM(centroids.shape, f32),
            flat,
            flat,
            pltpu.SemaphoreType.DMA((4,)),
        ],
        compiler_params=params(8),
        name="pack",
    )(chosen, in_hbm(centroids), vol, dens)
    received = lax.all_to_all(payload, AXES, split_axis=0, concat_axis=0, tiled=True)
    total, tiles, near, plan = pl.pallas_call(
        functools.partial(local_kernel, width),
        out_shape=(
            shape((blocks, ROWS, BLK), f32),
            pltpu.HBM((blocks + pairs, BLK, BLK), bf16),
            shape((blocks, FEATURES, BLK), bf16),
            shape((1 + 2 * longest,), i32),
        ),
        in_specs=[HBM, HBM, HBM, HBM, VMEM],
        out_specs=(VMEM, HBM, VMEM, SMEM),
        scratch_shapes=[
            row,
            row,
            pltpu.SMEM(pair_count.shape, i32),
            table,
            pltpu.VMEM((blocks + pairs, BLK, BLK), bf16),
            pltpu.VMEM((blocks, BLK, FEATURES), bf16),
            pltpu.VMEM((blocks, ROWS, BLK), bf16),
            square,
            results,
            results,
            pltpu.SemaphoreType.DMA((4,)),
            pltpu.SemaphoreType.DMA((blocks // width // DEPTH + 1,)),
            pltpu.SemaphoreType.DMA((pairs // width // DEPTH + 1,)),
        ],
        compiler_params=params(48),
        cost_estimate=pl.CostEstimate(
            flops=(blocks + pairs) * BLK * BLK * 100, bytes_accessed=1 << 20, transcendentals=0
        ),
        name="local",
    )(local_first, local_second, in_hbm(pair_count), chosen, words)
    received = received.reshape(peers * PEER_ROWS, HALF)
    filtered, ratio, payload2, *cross_tiles = pl.pallas_call(
        functools.partial(cross_kernel, width, keep),
        out_shape=(
            shape((flat_rows, HALF), f32),
            shape((blocks, ROWS, BLK), f32),
            shape((peers, 2 * slots, HALF), f32),
        )
        + ((pltpu.HBM((held, BLK, BLK), bf16),) if keep else ()),
        in_specs=[SMEM, HBM, VMEM, VMEM, VMEM, HBM],
        out_specs=(VMEM, VMEM, VMEM) + ((HBM,) if keep else ()),
        scratch_shapes=[
            ring,
            sums,
            flat,
            pltpu.VMEM((steps * width, ROWS, BLK), bf16),
            flat,
            table,
            square,
            results,
            pltpu.SemaphoreType.DMA((2,)),
        ]
        + ([ring_sems] if keep else []),
        compiler_params=params(48),
        name="cross",
    )(plan, chosen, received, near, total, sens)
    received2 = lax.all_to_all(payload2, AXES, split_axis=0, concat_axis=0, tiled=True)
    back = pl.pallas_call(
        functools.partial(back_local_kernel, BACK),
        out_shape=shape((blocks, ROWS, BLK), f32),
        in_specs=[HBM, HBM, VMEM, HBM],
        out_specs=VMEM,
        scratch_shapes=[
            row,
            row,
            pltpu.VMEM((blocks + pairs, BLK, BLK), bf16),
            pltpu.SemaphoreType.DMA((2,)),
            pltpu.SemaphoreType.DMA(((blocks + pairs) // LOAD,)),
        ],
        compiler_params=params(48),
        cost_estimate=pl.CostEstimate(
            flops=(blocks + pairs) * BLK * BLK * 100, bytes_accessed=1 << 20, transcendentals=0
        ),
        name="back_local",
    )(local_first, local_second, ratio, in_hbm(tiles))
    received2 = received2.reshape(places * 2, HALF)
    common = [sums, flat, pltpu.VMEM((places, BLK, BLK), bf16) if keep else ring]
    if keep:
        kernel, operands, specs = back_cross_kernel, (in_hbm(cross_tiles[0]),), [HBM]
        kernel = functools.partial(kernel, BACK, peers - 1)
        scratch = [pltpu.SMEM((1 + 2 * longest,), i32), pltpu.SemaphoreType.DMA((2,)), pltpu.SemaphoreType.DMA((places // LOAD,))]
    else:
        kernel, operands, specs = back_again_kernel, (received, near), [VMEM, VMEM]
        scratch = [square, pltpu.VMEM((steps * width, 1, BLK), f32), pltpu.SemaphoreType.DMA((1,))]
        kernel = functools.partial(kernel, width, slots)
    sensitivity = pl.pallas_call(
        kernel,
        out_shape=shape((flat_rows, HALF), f32),
        in_specs=[pl.BlockSpec(memory_space=pl.ANY) if keep else SMEM, VMEM, *specs, VMEM, HBM],
        out_specs=VMEM,
        scratch_shapes=common + scratch,
        compiler_params=params(48),
        name="back_cross",
    )(plan, received2, *operands, back, vol)
    return (filtered.reshape(-1), sensitivity.reshape(-1))


def solution(mesh):
    return jax.shard_map(
        shards,
        mesh=mesh,
        in_specs=(
            P(None, AXES),
            P(AXES),
            P(AXES),
            P(AXES),
            P(AXES),
            P(AXES),
            P(AXES, None),
            P(AXES, None, None),
        ),
        out_specs=(P(AXES), P(AXES)),
        check_vma=False,
    )
```

```python
import functools

import jax
import jax.numpy as jnp
from jax import lax
from jax.experimental import pallas as pl
from jax.experimental.pallas import tpu as pltpu
from jax.sharding import PartitionSpec as P

BLK = 256
HALF = BLK // 2
AXES = ("px", "py")
ROWS = 8
WORDS = 5
PEER_ROWS = 24
FEATURES = 32
COORD = 16384.0
VOLUME = 21845.0
DENSITY = 65535.0
MIDDLE = 1.5
TINY = 4e-6
STAY = 8
BACK = 16
LOAD = 4
WIDTH = 1
LOOK = 3
DEPTH = 20
KEEP_LIMIT = 20 << 20
MIB = 1 << 20

VMEM = pl.BlockSpec(memory_space=pltpu.VMEM)
SMEM = pl.BlockSpec(memory_space=pltpu.SMEM)
HBM = pl.BlockSpec(memory_space=pltpu.HBM)


def fixed(value, steps):
    return (value * steps + 0.5).astype(jnp.int32)


def two_halves(first, second):
    return first | (second << 16)


def pack_kernel(chosen_in, cent_in, vol_in, dens_in, payload, words, chosen, cent, vol, dens, sems):
    blocks = words.shape[0]
    waits = fetch(
        [(cent_in, cent), (vol_in, vol), (dens_in, dens), (chosen_in, chosen)], sems
    )
    words[...] = jnp.zeros_like(words)
    for wait in waits:
        wait()
    for b in range(blocks):
        low = cent[:, b * BLK : b * BLK + HALF]
        high = cent[:, b * BLK + HALF : (b + 1) * BLK]
        words[b, 0:3, :] = two_halves(fixed(low, COORD), fixed(high, COORD))
    for row, source, steps in ((3, vol, VOLUME), (4, dens, DENSITY)):
        low = source[pl.ds(0, blocks, stride=2), :]
        high = source[pl.ds(1, blocks, stride=2), :]
        words[:, row, :] = two_halves(fixed(low, steps), fixed(high, steps))
    slots, peers = chosen.shape

    def send(p, carry):
        for s in range(slots):
            payload[p, WORDS * s : WORDS * (s + 1), :] = words[chosen[s, p], 0:WORDS, :]
        return carry

    lax.fori_loop(0, peers, send, 0, unroll=4)


def decode(word):
    row = lax.broadcasted_iota(jnp.int32, (ROWS, BLK), 0)
    step = jnp.where(
        row < 3,
        1.0 / COORD,
        jnp.where(row == 3, 1.0 / VOLUME, jnp.where(row == 4, 1.0 / DENSITY, 0.0)),
    )
    parts = jnp.concatenate([word & 0xFFFF, lax.shift_right_logical(word, 16)], axis=1)
    held = parts.astype(jnp.float32) * step
    volume = held[3:4, :]
    values = jnp.where(row == 4, held * volume, held).astype(jnp.bfloat16)
    place = jnp.where(row < 3, held - MIDDLE, 0.0)
    high = place.astype(jnp.bfloat16).astype(jnp.float32)
    low = place - high
    norm = jnp.sum(place * place, axis=0, keepdims=True)
    norm1 = norm.astype(jnp.bfloat16).astype(jnp.float32)
    rest = norm - norm1
    norm2 = rest.astype(jnp.bfloat16).astype(jnp.float32)
    norm3 = rest - norm2
    one = jnp.where(row == 6, 1.0, 0.0)
    far1 = high + jnp.where(
        row == 3, norm1, jnp.where(row == 4, norm2, jnp.where(row == 5, norm3, one))
    )
    far2 = low + jnp.where((row == 3) | (row == 4), 1.0, 0.0)
    far = jnp.concatenate([far1, far2], axis=0).astype(jnp.bfloat16)
    far = jnp.concatenate([far, far], axis=0)
    near1 = -2.0 * high + jnp.where(
        (row >= 3) & (row <= 5), 1.0, jnp.where(row == 6, norm1, 0.0)
    )
    near2 = -2.0 * high + jnp.where(row == 3, norm2, jnp.where(row == 4, norm3, 0.0))
    near34 = -2.0 * low
    near = jnp.concatenate([near1, near2, near34, near34], axis=0).astype(jnp.bfloat16)
    return far, near, values


def product(rows, tile):
    return jnp.dot(rows, tile, preferred_element_type=jnp.float32)


def product_t(rows, tile):
    return lax.dot_general(
        rows, tile, (((1,), (1,)), ((), ())), preferred_element_type=jnp.float32
    )


def cone(squares, u):
    root = squares[u] * lax.rsqrt(jnp.maximum(squares[u], TINY))
    return jnp.maximum((1.0 - root).astype(jnp.bfloat16), 0)


def staged(groups, peel, width, tiles, kept, sems, squares, results, square, use, settle, beside=None):
    def place(d, u):
        return d % DEPTH * width + u

    def copy(k, count):
        part = pl.ds(k * DEPTH * width, count * width)
        return pltpu.make_async_copy(tiles.at[part], kept.at[part], sems.at[k])

    slots = LOOK + 1

    def distances(g, d):
        for u in range(width):
            squares[(d % slots) * width + u] = square(g * width + u, place(d, u))

    def cones(view, d):
        for u in range(width):
            view[d * width + u] = cone(squares, (d % slots) * width + u)

    def sums(view, g, d):
        for u in range(width):
            parts = use(g * width + u, place(d, u), view[d * width + u])
            for result, part in zip(results, parts):
                result[d * width + u] = part

    def settled(g, count):
        for d in range(count):
            for u in range(width):
                settle((g + d) * width + u, d * width + u)

    def view_from(g, count):
        return tiles.at[pl.ds(g * width, count * width)]

    for d in range(slots):
        distances(d, d)
    cones(view_from(0, 1), 0)
    turns = (groups - slots - peel) // DEPTH

    def steps(g, count):
        view = view_from(g, count + 1)
        for d in range(count):
            sums(view, g + d, d)
            distances(g + d + slots, d + slots)
            cones(view, d + 1)
        settled(g, count)

    def turn(k, carry):
        if beside is not None:
            beside(k)
        steps(k * DEPTH, DEPTH)
        if kept is not None:
            copy(k, DEPTH).start()
        return carry

    lax.fori_loop(0, turns, turn, 0)
    g = turns * DEPTH
    last = peel + slots
    view = view_from(g, last)
    for d in range(last):
        sums(view, g + d, d)
        if d < peel:
            distances(g + d + slots, d + slots)
        if d + 1 < last:
            cones(view, d + 1)
    if kept is not None:
        copy(turns, last).start()
    settled(g, last)

    def wait():
        def one(k, carry):
            copy(k, DEPTH).wait()
            return carry

        lax.fori_loop(0, turns, one, 0)
        copy(turns, last).wait()

    return wait


def peeled(most):
    return (most - LOOK - 1) % DEPTH


def padded(groups, peel):
    least = LOOK + 1 + peel
    return jnp.maximum((groups - least + DEPTH - 1) // DEPTH, 0) * DEPTH + least


def chunked(size, room, width, ring, squares, results, square, use, settle):
    def chunk(c, carry):
        base = c * room
        left = jnp.minimum(size - base, room)
        staged(
            padded((left + width - 1) // width, 0),
            0,
            width,
            ring,
            None,
            None,
            squares,
            results,
            lambda i, at: square(base + i, at),
            lambda i, at, tile: use(base + i, at, tile),
            lambda i, at: settle(jnp.where(i < left, base + i, size), at),
        )
        return carry

    lax.fori_loop(0, jnp.maximum((size + room - 1) // room, 1), chunk, 0)


def fetch(pairs, sems):
    copies = [pltpu.make_async_copy(a, b, sems.at[k]) for k, (a, b) in enumerate(pairs)]
    for copy in copies:
        copy.start()
    return [copy.wait for copy in copies]


def local_kernel(
    width, first_in, second_in, counts_in, chosen_in, words, total, kept, near, plan,
    first, second, counts, chosen, ring, far_t, vals, squares, sums0, sums1, sems, self_sems, pair_sems,
):
    blocks = words.shape[0]
    pairs = first.shape[0]
    peers = counts.shape[1]
    slots = chosen.shape[0]
    waits = fetch(
        [(first_in, first), (second_in, second), (counts_in, counts), (chosen_in, chosen)], sems
    )

    def square_self(b, at):
        f, n, v = decode(words[b])
        f = f.T
        far_t[b] = f
        near[b] = n
        vals[b] = v
        return product(f, n)

    def use_self(b, at, tile):
        return (product(vals[b], tile),)

    def settle_self(b, at):
        total[b] = sums0[at]

    part = pl.ds(0, blocks)
    wait_self = staged(
        blocks // width, peeled(blocks // width), width, ring.at[part], kept.at[part], self_sems, squares, (sums0,),
        square_self, use_self, settle_self,
    )
    for wait in waits:
        wait()

    def square_pair(j, at):
        return product(far_t[second[j]], near[first[j]])

    def use_pair(j, at, tile):
        return product(vals[second[j]], tile), product_t(vals[first[j]], tile)

    def settle_pair(j, at):
        total[first[j]] += sums0[at]
        total[second[j]] += sums1[at]

    length = plan_length(plan)
    turns = (pairs // width - LOOK - 1) // DEPTH
    share = -(-peers // turns)
    plan[0] = 0

    def collect(k):
        found = plan[0]
        for q in range(share):
            p = k * share + q
            peer = jnp.minimum(p, peers - 1)
            count = jnp.where(p < peers, counts[0, peer], 0)
            for s in range(slots):
                plan[1 + found] = peer * slots + s
                plan[1 + length + found] = chosen[s, peer]
                found = found + (s < count).astype(jnp.int32)
        plan[0] = found

    part = pl.ds(blocks, pairs)
    wait_pair = staged(
        pairs // width, peeled(pairs // width), width, ring.at[part], kept.at[part], pair_sems, squares, (sums0, sums1),
        square_pair, use_pair, settle_pair, collect,
    )

    for i in range(2 * DEPTH * width):
        plan[1 + plan[0] + i] = 0
        plan[1 + length + plan[0] + i] = 0
    wait_self()
    wait_pair()


def plan_length(plan):
    return (plan.shape[0] - 1) // 2


def far_word(received, slots, place):
    peer, slot = place // slots, place % slots
    return received[pl.ds(peer * PEER_ROWS + slot * WORDS, ROWS), :]


def cross_kernel(
    width, keep, plan, chosen_in, received, near, total_in, sens_in, filtered, ratio, payload, *rest
):
    kept = None
    if keep:
        kept, stay, *rest = rest
    ring, total, vals, sens, chosen, squares, sums0, sems, *ring_sems = rest
    blocks = near.shape[0]
    waits = fetch([(chosen_in, chosen), (sens_in, sens)], sems)
    total[...] = total_in[...]
    slots, peers = chosen.shape
    size, length = plan[0], plan_length(plan)

    def square(i, at):
        f, unused, v = decode(far_word(received, slots, plan[1 + i]))
        vals[at] = v
        return product(f.T, near[plan[1 + length + i]])

    def use(i, at, tile):
        return (product(vals[at], tile),)

    def settle(i, at):
        total[plan[1 + length + i]] += jnp.where(i < size, sums0[at], 0.0)

    if keep:
        peel = peeled((peers - 1) * slots // width)
        groups = padded((size + width - 1) // width, peel)
        wait_tiles = staged(
            groups, peel, width, ring, kept, ring_sems[0], squares, (sums0,), square, use, settle
        )
    else:
        room = ring.shape[0] - (DEPTH + LOOK + 1) * width
        chunked(size, room, width, ring, squares, (sums0,), square, use, settle)
    if keep:
        waits += fetch([(ring.at[pl.ds(0, stay.shape[0])], stay)], ring_sems[1])
    for wait in waits:
        wait()
    base = total[:, 3, :]
    filt = total[:, 4, :] / base
    for half in range(2):
        rows = pl.ds(half, blocks, stride=2)
        lanes = slice(half * HALF, (half + 1) * HALF)
        filtered[rows, :] = filt[:, lanes]
        part = sens[rows, :] / base[:, lanes]
        ratio[rows, :] = part.astype(jnp.bfloat16).astype(jnp.float32)
    def send(p, carry):
        for s in range(slots):
            payload[p, 2 * s : 2 * s + 2, :] = ratio[pl.ds(2 * chosen[s, p], 2), :]
        return carry

    lax.fori_loop(0, peers, send, 0, unroll=4)
    if keep:
        wait_tiles()


def tile_loads(width, kept, tiles, sems):
    each = width // LOAD

    def copy(k):
        part = pl.ds(k * LOAD, LOAD)
        return pltpu.make_async_copy(kept.at[part], tiles.at[part], sems.at[k])

    def start(a, b):
        def one(k, carry):
            copy(k).start()
            return carry

        lax.fori_loop(a // LOAD, b // LOAD, one, 0)

    def ready(k, u=0):
        for j in range(u // LOAD, each):
            copy(k * each + j).wait()

    return start, ready


def back_local_kernel(
    width, first_in, second_in, ratio, kept, total, first, second, tiles, sems, tile_sems
):
    blocks = total.shape[0]
    pairs = first.shape[0]
    start, ready = tile_loads(width, kept, tiles, tile_sems)
    waits = fetch([(first_in, first), (second_in, second)], sems)
    start(blocks, blocks + pairs)
    start(0, blocks)
    total[...] = jnp.zeros_like(total)

    def rows(b):
        return far_ratio(ratio, b)

    for wait in waits:
        wait()

    def pair(k, carry):
        ready(blocks // width + k)
        ids = [(first[k * width + u], second[k * width + u]) for u in range(width)]
        sums = []
        for u, (a, b) in enumerate(ids):
            tile = tiles[blocks + k * width + u]
            sums.append((product(rows(b), tile), product_t(rows(a), tile)))
        for (a, b), (to_first, to_second) in zip(ids, sums):
            total[a, 0:1, :] += to_first
            total[b, 0:1, :] += to_second
        return carry

    lax.fori_loop(0, pairs // width, pair, 0)

    def own(k, carry):
        ready(k)
        sums = [product(rows(k * width + u), tiles[k * width + u]) for u in range(width)]
        for u in range(width):
            total[k * width + u, 0:1, :] += sums[u]
        return carry

    lax.fori_loop(0, blocks // width, own, 0)


def far_ratio(ratio, place):
    row0 = ratio[pl.ds(place * 2, 1), :]
    row1 = ratio[pl.ds(place * 2 + 1, 1), :]
    return jnp.concatenate([row0, row1], axis=1).astype(jnp.bfloat16)


def finish_back(blocks, vol, total, out):
    for half in range(2):
        rows = pl.ds(half, blocks, stride=2)
        lanes = slice(half * HALF, (half + 1) * HALF)
        out[rows, :] = vol[rows, :] * total[:, 0, lanes]


def back_cross_kernel(
    width, least, plan_in, ratio, kept, stay, total_in, vol_in, out,
    total, vol, tiles, plan, sems, tile_sems,
):
    blocks = total.shape[0]
    start, ready = tile_loads(width, kept, tiles, tile_sems)
    wait_plan, *waits = fetch([(plan_in, plan), (vol_in, vol)], sems)
    early = -(-least // width) * width
    staying = stay.shape[0]
    start(staying, early)
    total[...] = total_in[...]
    wait_plan()
    size, length = plan[0], plan_length(plan)
    groups = (size + width - 1) // width
    start(early, groups * width)

    def group(k, tile):
        sums = []
        for u in range(width):
            i = k * width + u
            part = product(far_ratio(ratio, plan[1 + i]), tile(u, i))
            part = jnp.where(i < size, part, 0.0)
            sums.append((plan[1 + length + i], part))
        for b, part in sums:
            total[b, 0:1, :] += part

    def turn(k, carry):
        ready(k)
        group(k, lambda u, i: tiles[i])
        return carry

    ready(0, staying)
    group(0, lambda u, i: stay[i] if u < staying else tiles[i])
    lax.fori_loop(1, groups, turn, 0)
    for wait in waits:
        wait()
    finish_back(blocks, vol, total, out)


def back_again_kernel(
    width, slots, plan, ratio, received, near, total_in, vol_in, out,
    total, vol, ring, squares, sums0, sems,
):
    blocks = total.shape[0]
    waits = fetch([(vol_in, vol)], sems)
    total[...] = total_in[...]
    size, length = plan[0], plan_length(plan)

    def square(i, at):
        f, unused, v = decode(far_word(received, slots, plan[1 + i]))
        return product(f.T, near[plan[1 + length + i]])

    def use(i, at, tile):
        return (product(far_ratio(ratio, plan[1 + i]), tile),)

    def settle(i, at):
        total[plan[1 + length + i], 0:1, :] += jnp.where(i < size, sums0[at], 0.0)

    room = ring.shape[0] - (DEPTH + LOOK + 1) * width
    chunked(size, room, width, ring, squares, (sums0,), square, use, settle)
    for wait in waits:
        wait()
    finish_back(blocks, vol, total, out)


def in_vmem(array):
    return pltpu.with_memory_space_constraint(array, pltpu.VMEM)


def in_hbm(array):
    return pltpu.with_memory_space_constraint(array, pltpu.HBM)


def params(mib):
    return pltpu.CompilerParams(vmem_limit_bytes=mib * MIB)


def shards(
    centroids, volumes, densities, sens_in, local_first, local_second, pair_count, pair_mine
):
    elements = volumes.shape[0]
    blocks = elements // BLK
    flat_rows = elements // HALF
    vol = in_hbm(volumes.reshape(flat_rows, HALF))
    dens = in_hbm(densities.reshape(flat_rows, HALF))
    sens = in_hbm(sens_in.reshape(flat_rows, HALF))
    local_first, local_second = in_hbm(local_first), in_hbm(local_second)
    chosen = in_hbm(pair_mine[0].T)
    slots, peers = chosen.shape
    places = peers * slots
    pairs = local_first.shape[0]
    longest = 2 * places
    f32, bf16, i32 = jnp.float32, jnp.bfloat16, jnp.int32
    shape = jax.ShapeDtypeStruct
    width = WIDTH
    flat = pltpu.VMEM((flat_rows, HALF), f32)
    sums = pltpu.VMEM((blocks, ROWS, BLK), f32)
    square = pltpu.VMEM(((LOOK + 1) * width, BLK, BLK), f32)
    tile_bytes = BLK * BLK * 2
    keep = places * tile_bytes <= KEEP_LIMIT
    most = (places - slots) // width
    turns = most // DEPTH
    held = max(most * width, -(-most * width // BACK) * BACK)
    ring = pltpu.VMEM((held if keep else KEEP_LIMIT // tile_bytes, BLK, BLK), bf16)
    steps = DEPTH + LOOK + 1
    results = pltpu.VMEM((steps * width, ROWS, BLK), f32)
    ring_sems = pltpu.SemaphoreType.DMA((turns + 1,))
    table = pltpu.SMEM(chosen.shape, i32)
    row = pltpu.SMEM((pairs,), i32)

    payload, words = pl.pallas_call(
        pack_kernel,
        out_shape=(shape((peers, PEER_ROWS, HALF), i32), shape((blocks, ROWS, HALF), i32)),
        in_specs=[HBM] * 4,
        out_specs=(VMEM, VMEM),
        scratch_shapes=[
            table,
            pltpu.VMEM(centroids.shape, f32),
            flat,
            flat,
            pltpu.SemaphoreType.DMA((4,)),
        ],
        compiler_params=params(8),
        name="pack",
    )(chosen, in_hbm(centroids), vol, dens)
    received = lax.all_to_all(payload, AXES, split_axis=0, concat_axis=0, tiled=True)
    total, tiles, near, plan = pl.pallas_call(
        functools.partial(local_kernel, width),
        out_shape=(
            shape((blocks, ROWS, BLK), f32),
            pltpu.HBM((blocks + pairs, BLK, BLK), bf16),
            shape((blocks, FEATURES, BLK), bf16),
            shape((1 + 2 * longest,), i32),
        ),
        in_specs=[HBM, HBM, HBM, HBM, VMEM],
        out_specs=(VMEM, HBM, VMEM, SMEM),
        scratch_shapes=[
            row,
            row,
            pltpu.SMEM(pair_count.shape, i32),
            table,
            pltpu.VMEM((blocks + pairs, BLK, BLK), bf16),
            pltpu.VMEM((blocks, BLK, FEATURES), bf16),
            pltpu.VMEM((blocks, ROWS, BLK), bf16),
            square,
            results,
            results,
            pltpu.SemaphoreType.DMA((4,)),
            pltpu.SemaphoreType.DMA((blocks // width // DEPTH + 1,)),
            pltpu.SemaphoreType.DMA((pairs // width // DEPTH + 1,)),
        ],
        compiler_params=params(48),
        cost_estimate=pl.CostEstimate(
            flops=(blocks + pairs) * BLK * BLK * 100, bytes_accessed=1 << 20, transcendentals=0
        ),
        name="local",
    )(local_first, local_second, in_hbm(pair_count), chosen, words)
    received = received.reshape(peers * PEER_ROWS, HALF)
    filtered, ratio, payload2, *cross_tiles = pl.pallas_call(
        functools.partial(cross_kernel, width, keep),
        out_shape=(
            shape((flat_rows, HALF), f32),
            shape((flat_rows, HALF), f32),
            shape((peers, 2 * slots, HALF), f32),
        )
        + ((pltpu.HBM((held, BLK, BLK), bf16), pltpu.VMEM((STAY, BLK, BLK), bf16)) if keep else ()),
        in_specs=[SMEM, HBM, VMEM, VMEM, VMEM, HBM],
        out_specs=(VMEM, VMEM, VMEM) + ((HBM, VMEM) if keep else ()),
        scratch_shapes=[
            ring,
            sums,
            pltpu.VMEM((steps * width, ROWS, BLK), bf16),
            flat,
            table,
            square,
            results,
            pltpu.SemaphoreType.DMA((2,)),
        ]
        + ([ring_sems, pltpu.SemaphoreType.DMA((1,))] if keep else []),
        compiler_params=params(48),
        name="cross",
    )(plan, chosen, received, near, total, sens)
    received2 = lax.all_to_all(payload2, AXES, split_axis=0, concat_axis=0, tiled=True)
    back = pl.pallas_call(
        functools.partial(back_local_kernel, BACK),
        out_shape=shape((blocks, ROWS, BLK), f32),
        in_specs=[HBM, HBM, VMEM, HBM],
        out_specs=VMEM,
        scratch_shapes=[
            row,
            row,
            pltpu.VMEM((blocks + pairs, BLK, BLK), bf16),
            pltpu.SemaphoreType.DMA((2,)),
            pltpu.SemaphoreType.DMA(((blocks + pairs) // LOAD,)),
        ],
        compiler_params=params(48),
        cost_estimate=pl.CostEstimate(
            flops=(blocks + pairs) * BLK * BLK * 100, bytes_accessed=1 << 20, transcendentals=0
        ),
        name="back_local",
    )(local_first, local_second, ratio, in_hbm(tiles))
    received2 = received2.reshape(places * 2, HALF)
    common = [sums, flat, pltpu.VMEM((places, BLK, BLK), bf16) if keep else ring]
    if keep:
        kernel, operands, specs = back_cross_kernel, (in_hbm(cross_tiles[0]), in_vmem(cross_tiles[1])), [HBM, VMEM]
        kernel = functools.partial(kernel, BACK, peers - 1)
        scratch = [pltpu.SMEM((1 + 2 * longest,), i32), pltpu.SemaphoreType.DMA((2,)), pltpu.SemaphoreType.DMA((places // LOAD,))]
    else:
        kernel, operands, specs = back_again_kernel, (received, near), [VMEM, VMEM]
        scratch = [square, pltpu.VMEM((steps * width, 1, BLK), f32), pltpu.SemaphoreType.DMA((1,))]
        kernel = functools.partial(kernel, width, slots)
    sensitivity = pl.pallas_call(
        kernel,
        out_shape=shape((flat_rows, HALF), f32),
        in_specs=[pl.BlockSpec(memory_space=pl.ANY) if keep else SMEM, VMEM, *specs, VMEM, HBM],
        out_specs=VMEM,
        scratch_shapes=common + scratch,
        compiler_params=params(48),
        name="back_cross",
    )(plan, received2, *operands, back, vol)
    return (filtered.reshape(-1), sensitivity.reshape(-1))


def solution(mesh):
    return jax.shard_map(
        shards,
        mesh=mesh,
        in_specs=(
            P(None, AXES),
            P(AXES),
            P(AXES),
            P(AXES),
            P(AXES),
            P(AXES),
            P(AXES, None),
            P(AXES, None, None),
        ),
        out_specs=(P(AXES), P(AXES)),
        check_vma=False,
    )
```

```python
import functools

import jax
import jax.numpy as jnp
from jax import lax
from jax.experimental import pallas as pl
from jax.experimental.pallas import tpu as pltpu
from jax.sharding import PartitionSpec as P

BLK = 256
HALF = BLK // 2
AXES = ("px", "py")
ROWS = 8
WORDS = 5
PEER_ROWS = 24
FEATURES = 32
COORD = 16384.0
VOLUME = 21845.0
DENSITY = 65535.0
MIDDLE = 1.5
TINY = 4e-6
BACK = 16
LOAD = 4
WIDTH = 1
LOOK = 3
DEPTH = 12
KEEP_LIMIT = 20 << 20
MIB = 1 << 20

VMEM = pl.BlockSpec(memory_space=pltpu.VMEM)
SMEM = pl.BlockSpec(memory_space=pltpu.SMEM)
HBM = pl.BlockSpec(memory_space=pltpu.HBM)


def fixed(value, steps):
    return (value * steps + 0.5).astype(jnp.int32)


def two_halves(first, second):
    return first | (second << 16)


def pack_kernel(chosen_in, cent_in, vol_in, dens_in, payload, words, chosen, cent, vol, dens, sems):
    blocks = words.shape[0]
    waits = fetch(
        [(cent_in, cent), (vol_in, vol), (dens_in, dens), (chosen_in, chosen)], sems
    )
    words[...] = jnp.zeros_like(words)
    for wait in waits:
        wait()
    for b in range(blocks):
        low = cent[:, b * BLK : b * BLK + HALF]
        high = cent[:, b * BLK + HALF : (b + 1) * BLK]
        words[b, 0:3, :] = two_halves(fixed(low, COORD), fixed(high, COORD))
    for row, source, steps in ((3, vol, VOLUME), (4, dens, DENSITY)):
        low = source[pl.ds(0, blocks, stride=2), :]
        high = source[pl.ds(1, blocks, stride=2), :]
        words[:, row, :] = two_halves(fixed(low, steps), fixed(high, steps))
    slots, peers = chosen.shape

    def send(p, carry):
        for s in range(slots):
            payload[p, WORDS * s : WORDS * (s + 1), :] = words[chosen[s, p], 0:WORDS, :]
        return carry

    lax.fori_loop(0, peers, send, 0, unroll=4)


def decode(word):
    row = lax.broadcasted_iota(jnp.int32, (ROWS, BLK), 0)
    step = jnp.where(
        row < 3,
        1.0 / COORD,
        jnp.where(row == 3, 1.0 / VOLUME, jnp.where(row == 4, 1.0 / DENSITY, 0.0)),
    )
    parts = jnp.concatenate([word & 0xFFFF, lax.shift_right_logical(word, 16)], axis=1)
    held = parts.astype(jnp.float32) * step
    volume = held[3:4, :]
    values = jnp.where(row == 4, held * volume, held).astype(jnp.bfloat16)
    place = jnp.where(row < 3, held - MIDDLE, 0.0)
    high = place.astype(jnp.bfloat16).astype(jnp.float32)
    low = place - high
    norm = jnp.sum(place * place, axis=0, keepdims=True)
    norm1 = norm.astype(jnp.bfloat16).astype(jnp.float32)
    rest = norm - norm1
    norm2 = rest.astype(jnp.bfloat16).astype(jnp.float32)
    norm3 = rest - norm2
    one = jnp.where(row == 6, 1.0, 0.0)
    far1 = high + jnp.where(
        row == 3, norm1, jnp.where(row == 4, norm2, jnp.where(row == 5, norm3, one))
    )
    far2 = low + jnp.where((row == 3) | (row == 4), 1.0, 0.0)
    far = jnp.concatenate([far1, far2], axis=0).astype(jnp.bfloat16)
    far = jnp.concatenate([far, far], axis=0)
    near1 = -2.0 * high + jnp.where(
        (row >= 3) & (row <= 5), 1.0, jnp.where(row == 6, norm1, 0.0)
    )
    near2 = -2.0 * high + jnp.where(row == 3, norm2, jnp.where(row == 4, norm3, 0.0))
    near34 = -2.0 * low
    near = jnp.concatenate([near1, near2, near34, near34], axis=0).astype(jnp.bfloat16)
    return far, near, values


def product(rows, tile):
    return jnp.dot(rows, tile, preferred_element_type=jnp.float32)


def product_t(rows, tile):
    return lax.dot_general(
        rows, tile, (((1,), (1,)), ((), ())), preferred_element_type=jnp.float32
    )


def cone(squares, u):
    root = squares[u] * lax.rsqrt(jnp.maximum(squares[u], TINY))
    return jnp.maximum((1.0 - root).astype(jnp.bfloat16), 0)


def staged(groups, peel, width, tiles, kept, sems, squares, results, square, use, settle, beside=None):
    def place(d, u):
        return d % DEPTH * width + u

    def copy(k, count):
        part = pl.ds(k * DEPTH * width, count * width)
        return pltpu.make_async_copy(tiles.at[part], kept.at[part], sems.at[k])

    slots = LOOK + 1

    def distances(g, d):
        for u in range(width):
            squares[(d % slots) * width + u] = square(g * width + u, place(d, u))

    def cones(view, d):
        for u in range(width):
            view[d * width + u] = cone(squares, (d % slots) * width + u)

    def sums(view, g, d):
        for u in range(width):
            parts = use(g * width + u, place(d, u), view[d * width + u])
            for result, part in zip(results, parts):
                result[d * width + u] = part

    def settled(g, count):
        for d in range(count):
            for u in range(width):
                settle((g + d) * width + u, d * width + u)

    def view_from(g, count):
        return tiles.at[pl.ds(g * width, count * width)]

    for d in range(slots):
        distances(d, d)
    cones(view_from(0, 1), 0)
    turns = (groups - slots - peel) // DEPTH

    def steps(g, count):
        view = view_from(g, count + 1)
        for d in range(count):
            sums(view, g + d, d)
            distances(g + d + slots, d + slots)
            cones(view, d + 1)
        settled(g, count)

    def turn(k, carry):
        if beside is not None:
            beside(k)
        steps(k * DEPTH, DEPTH)
        if kept is not None:
            copy(k, DEPTH).start()
        return carry

    lax.fori_loop(0, turns, turn, 0)
    g = turns * DEPTH
    last = peel + slots
    view = view_from(g, last)
    for d in range(last):
        sums(view, g + d, d)
        if d < peel:
            distances(g + d + slots, d + slots)
        if d + 1 < last:
            cones(view, d + 1)
    if kept is not None:
        copy(turns, last).start()
    settled(g, last)

    def wait():
        def one(k, carry):
            copy(k, DEPTH).wait()
            return carry

        lax.fori_loop(0, turns, one, 0)
        copy(turns, last).wait()

    return wait


def peeled(most):
    return (most - LOOK - 1) % DEPTH


def padded(groups, peel):
    least = LOOK + 1 + peel
    return jnp.maximum((groups - least + DEPTH - 1) // DEPTH, 0) * DEPTH + least


def chunked(size, room, width, ring, squares, results, square, use, settle):
    def chunk(c, carry):
        base = c * room
        left = jnp.minimum(size - base, room)
        staged(
            padded((left + width - 1) // width, 0),
            0,
            width,
            ring,
            None,
            None,
            squares,
            results,
            lambda i, at: square(base + i, at),
            lambda i, at, tile: use(base + i, at, tile),
            lambda i, at: settle(jnp.where(i < left, base + i, size), at),
        )
        return carry

    lax.fori_loop(0, jnp.maximum((size + room - 1) // room, 1), chunk, 0)


def fetch(pairs, sems):
    copies = [pltpu.make_async_copy(a, b, sems.at[k]) for k, (a, b) in enumerate(pairs)]
    for copy in copies:
        copy.start()
    return [copy.wait for copy in copies]


def local_kernel(
    width, first_in, second_in, counts_in, chosen_in, words, total, kept, near, plan,
    first, second, counts, chosen, ring, far_t, vals, squares, sums0, sums1, sems, self_sems, pair_sems,
):
    blocks = words.shape[0]
    pairs = first.shape[0]
    peers = counts.shape[1]
    slots = chosen.shape[0]
    waits = fetch(
        [(first_in, first), (second_in, second), (counts_in, counts), (chosen_in, chosen)], sems
    )

    def square_self(b, at):
        f, n, v = decode(words[b])
        f = f.T
        far_t[b] = f
        near[b] = n
        vals[b] = v
        return product(f, n)

    def use_self(b, at, tile):
        return (product(vals[b], tile),)

    def settle_self(b, at):
        total[b] = sums0[at]

    part = pl.ds(0, blocks)
    wait_self = staged(
        blocks // width, peeled(blocks // width), width, ring.at[part], kept.at[part], self_sems, squares, (sums0,),
        square_self, use_self, settle_self,
    )
    for wait in waits:
        wait()

    def square_pair(j, at):
        return product(far_t[second[j]], near[first[j]])

    def use_pair(j, at, tile):
        return product(vals[second[j]], tile), product_t(vals[first[j]], tile)

    def settle_pair(j, at):
        total[first[j]] += sums0[at]
        total[second[j]] += sums1[at]

    length = plan_length(plan)
    turns = (pairs // width - LOOK - 1) // DEPTH
    share = -(-peers // turns)
    plan[0] = 0

    def collect(k):
        found = plan[0]
        for q in range(share):
            p = k * share + q
            peer = jnp.minimum(p, peers - 1)
            count = jnp.where(p < peers, counts[0, peer], 0)
            for s in range(slots):
                plan[1 + found] = peer * slots + s
                plan[1 + length + found] = chosen[s, peer]
                found = found + (s < count).astype(jnp.int32)
        plan[0] = found

    part = pl.ds(blocks, pairs)
    wait_pair = staged(
        pairs // width, peeled(pairs // width), width, ring.at[part], kept.at[part], pair_sems, squares, (sums0, sums1),
        square_pair, use_pair, settle_pair, collect,
    )

    for i in range(2 * DEPTH * width):
        plan[1 + plan[0] + i] = 0
        plan[1 + length + plan[0] + i] = 0
    wait_self()
    wait_pair()


def plan_length(plan):
    return (plan.shape[0] - 1) // 2


def far_word(received, slots, place):
    peer, slot = place // slots, place % slots
    return received[pl.ds(peer * PEER_ROWS + slot * WORDS, ROWS), :]


def cross_kernel(
    width, keep, plan, chosen_in, received, near, total_in, sens_in, filtered, ratio, payload, *rest
):
    kept = None
    if keep:
        kept, *rest = rest
    ring, total, flat, vals, sens, chosen, squares, sums0, sends, filts, sems, out_sems, *ring_sems = rest
    blocks = near.shape[0]
    waits = fetch([(chosen_in, chosen), (sens_in, sens)], sems)
    total[...] = total_in[...]
    slots, peers = chosen.shape
    size, length = plan[0], plan_length(plan)

    def square(i, at):
        f, unused, v = decode(far_word(received, slots, plan[1 + i]))
        vals[at] = v
        return product(f.T, near[plan[1 + length + i]])

    def use(i, at, tile):
        return (product(vals[at], tile),)

    def settle(i, at):
        total[plan[1 + length + i]] += jnp.where(i < size, sums0[at], 0.0)

    if keep:
        peel = peeled((peers - 1) * slots // width)
        groups = padded((size + width - 1) // width, peel)
        wait_tiles = staged(
            groups, peel, width, ring, kept, ring_sems[0], squares, (sums0,), square, use, settle
        )
    else:
        room = ring.shape[0] - (DEPTH + LOOK + 1) * width
        chunked(size, room, width, ring, squares, (sums0,), square, use, settle)
    for wait in waits:
        wait()
    base = total[:, 3, :]
    for half in range(2):
        rows = pl.ds(half, blocks, stride=2)
        part = sens[rows, :] / base[:, half * HALF : (half + 1) * HALF]
        flat[rows, :] = part.astype(jnp.bfloat16).astype(jnp.float32)

    def send(p, carry):
        for s in range(slots):
            sends[p, 2 * s : 2 * s + 2, :] = flat[pl.ds(2 * chosen[s, p], 2), :]
        return carry

    lax.fori_loop(0, peers, send, 0, unroll=4)
    sent = pltpu.make_async_copy(sends, payload, out_sems.at[0])
    sent.start()
    filt = total[:, 4, :] / base
    ratio[...] = jnp.zeros_like(ratio)
    for half in range(2):
        rows = pl.ds(half, blocks, stride=2)
        lanes = slice(half * HALF, (half + 1) * HALF)
        filts[rows, :] = filt[:, lanes]
        ratio[:, 0, lanes] = flat[rows, :]
    written = pltpu.make_async_copy(filts, filtered, out_sems.at[1])
    written.start()
    if keep:
        wait_tiles()
    sent.wait()
    written.wait()


def tile_loads(width, kept, tiles, sems):
    each = width // LOAD

    def copy(k):
        part = pl.ds(k * LOAD, LOAD)
        return pltpu.make_async_copy(kept.at[part], tiles.at[part], sems.at[k])

    def start(a, b):
        def one(k, carry):
            copy(k).start()
            return carry

        lax.fori_loop(a * each, b * each, one, 0)

    def ready(k):
        for j in range(each):
            copy(k * each + j).wait()

    return start, ready


def back_local_kernel(
    width, first_in, second_in, ratio, kept, total, first, second, tiles, sems, tile_sems
):
    blocks = ratio.shape[0]
    pairs = first.shape[0]
    start, ready = tile_loads(width, kept, tiles, tile_sems)
    waits = fetch([(first_in, first), (second_in, second)], sems)
    start(blocks // width, (blocks + pairs) // width)
    start(0, blocks // width)
    total[...] = jnp.zeros_like(total)

    def rows(b):
        return ratio[b].astype(jnp.bfloat16)

    for wait in waits:
        wait()

    def pair(k, carry):
        ready(blocks // width + k)
        ids = [(first[k * width + u], second[k * width + u]) for u in range(width)]
        sums = []
        for u, (a, b) in enumerate(ids):
            tile = tiles[blocks + k * width + u]
            sums.append((product(rows(b), tile), product_t(rows(a), tile)))
        for (a, b), (to_first, to_second) in zip(ids, sums):
            total[a] += to_first
            total[b] += to_second
        return carry

    lax.fori_loop(0, pairs // width, pair, 0)

    def own(k, carry):
        ready(k)
        sums = [product(rows(k * width + u), tiles[k * width + u]) for u in range(width)]
        for u in range(width):
            total[k * width + u] += sums[u]
        return carry

    lax.fori_loop(0, blocks // width, own, 0)


def far_ratio(ratio, place):
    row0 = ratio[pl.ds(place * 2, 1), :]
    row1 = ratio[pl.ds(place * 2 + 1, 1), :]
    return jnp.concatenate([row0, row1], axis=1).astype(jnp.bfloat16)


def finish_back(blocks, vol, total, out):
    for half in range(2):
        rows = pl.ds(half, blocks, stride=2)
        lanes = slice(half * HALF, (half + 1) * HALF)
        out[rows, :] = vol[rows, :] * total[:, 0, lanes]


def back_cross_kernel(
    width, least, plan_in, ratio, kept, total_in, vol_in, out,
    total, vol, tiles, plan, sems, tile_sems,
):
    blocks = total.shape[0]
    start, ready = tile_loads(width, kept, tiles, tile_sems)
    wait_plan, *waits = fetch([(plan_in, plan), (vol_in, vol)], sems)
    early = -(-least // width)
    start(0, early)
    total[...] = total_in[...]
    wait_plan()
    size, length = plan[0], plan_length(plan)
    groups = (size + width - 1) // width
    start(early, groups)

    def turn(k, carry):
        ready(k)
        sums = []
        for u in range(width):
            i = k * width + u
            part = product(far_ratio(ratio, plan[1 + i]), tiles[i])
            part = jnp.where(i < size, part, 0.0)
            sums.append((plan[1 + length + i], part))
        for b, part in sums:
            total[b, 0:1, :] += part
        return carry

    lax.fori_loop(0, groups, turn, 0)
    for wait in waits:
        wait()
    finish_back(blocks, vol, total, out)


def back_again_kernel(
    width, slots, plan, ratio, received, near, total_in, vol_in, out,
    total, vol, ring, squares, sums0, sems,
):
    blocks = total.shape[0]
    waits = fetch([(vol_in, vol)], sems)
    total[...] = total_in[...]
    size, length = plan[0], plan_length(plan)

    def square(i, at):
        f, unused, v = decode(far_word(received, slots, plan[1 + i]))
        return product(f.T, near[plan[1 + length + i]])

    def use(i, at, tile):
        return (product(far_ratio(ratio, plan[1 + i]), tile),)

    def settle(i, at):
        total[plan[1 + length + i], 0:1, :] += jnp.where(i < size, sums0[at], 0.0)

    room = ring.shape[0] - (DEPTH + LOOK + 1) * width
    chunked(size, room, width, ring, squares, (sums0,), square, use, settle)
    for wait in waits:
        wait()
    finish_back(blocks, vol, total, out)


def in_hbm(array):
    return pltpu.with_memory_space_constraint(array, pltpu.HBM)


def params(mib):
    return pltpu.CompilerParams(vmem_limit_bytes=mib * MIB)


def shards(
    centroids, volumes, densities, sens_in, local_first, local_second, pair_count, pair_mine
):
    elements = volumes.shape[0]
    blocks = elements // BLK
    flat_rows = elements // HALF
    vol = in_hbm(volumes.reshape(flat_rows, HALF))
    dens = in_hbm(densities.reshape(flat_rows, HALF))
    sens = in_hbm(sens_in.reshape(flat_rows, HALF))
    local_first, local_second = in_hbm(local_first), in_hbm(local_second)
    chosen = in_hbm(pair_mine[0].T)
    slots, peers = chosen.shape
    places = peers * slots
    pairs = local_first.shape[0]
    longest = 2 * places
    f32, bf16, i32 = jnp.float32, jnp.bfloat16, jnp.int32
    shape = jax.ShapeDtypeStruct
    width = WIDTH
    flat = pltpu.VMEM((flat_rows, HALF), f32)
    sums = pltpu.VMEM((blocks, ROWS, BLK), f32)
    square = pltpu.VMEM(((LOOK + 1) * width, BLK, BLK), f32)
    tile_bytes = BLK * BLK * 2
    keep = places * tile_bytes <= KEEP_LIMIT
    most = (places - slots) // width
    turns = most // DEPTH
    held = max(most * width, -(-most * width // BACK) * BACK)
    ring = pltpu.VMEM((held if keep else KEEP_LIMIT // tile_bytes, BLK, BLK), bf16)
    steps = DEPTH + LOOK + 1
    results = pltpu.VMEM((steps * width, ROWS, BLK), f32)
    ring_sems = pltpu.SemaphoreType.DMA((turns + 1,))
    table = pltpu.SMEM(chosen.shape, i32)
    row = pltpu.SMEM((pairs,), i32)

    payload, words = pl.pallas_call(
        pack_kernel,
        out_shape=(shape((peers, PEER_ROWS, HALF), i32), shape((blocks, ROWS, HALF), i32)),
        in_specs=[HBM] * 4,
        out_specs=(VMEM, VMEM),
        scratch_shapes=[
            table,
            pltpu.VMEM(centroids.shape, f32),
            flat,
            flat,
            pltpu.SemaphoreType.DMA((4,)),
        ],
        compiler_params=params(8),
        name="pack",
    )(chosen, in_hbm(centroids), vol, dens)
    received = lax.all_to_all(payload, AXES, split_axis=0, concat_axis=0, tiled=True)
    total, tiles, near, plan = pl.pallas_call(
        functools.partial(local_kernel, width),
        out_shape=(
            shape((blocks, ROWS, BLK), f32),
            pltpu.HBM((blocks + pairs, BLK, BLK), bf16),
            shape((blocks, FEATURES, BLK), bf16),
            shape((1 + 2 * longest,), i32),
        ),
        in_specs=[HBM, HBM, HBM, HBM, VMEM],
        out_specs=(VMEM, HBM, VMEM, SMEM),
        scratch_shapes=[
            row,
            row,
            pltpu.SMEM(pair_count.shape, i32),
            table,
            pltpu.VMEM((blocks + pairs, BLK, BLK), bf16),
            pltpu.VMEM((blocks, BLK, FEATURES), bf16),
            pltpu.VMEM((blocks, ROWS, BLK), bf16),
            square,
            results,
            results,
            pltpu.SemaphoreType.DMA((4,)),
            pltpu.SemaphoreType.DMA((blocks // width // DEPTH + 1,)),
            pltpu.SemaphoreType.DMA((pairs // width // DEPTH + 1,)),
        ],
        compiler_params=params(48),
        cost_estimate=pl.CostEstimate(
            flops=(blocks + pairs) * BLK * BLK * 100, bytes_accessed=1 << 20, transcendentals=0
        ),
        name="local",
    )(local_first, local_second, in_hbm(pair_count), chosen, words)
    received = received.reshape(peers * PEER_ROWS, HALF)
    filtered, ratio, payload2, *cross_tiles = pl.pallas_call(
        functools.partial(cross_kernel, width, keep),
        out_shape=(
            pltpu.HBM((flat_rows, HALF), f32),
            shape((blocks, ROWS, BLK), f32),
            pltpu.HBM((peers, 2 * slots, HALF), f32),
        )
        + ((pltpu.HBM((held, BLK, BLK), bf16),) if keep else ()),
        in_specs=[SMEM, HBM, VMEM, VMEM, VMEM, HBM],
        out_specs=(HBM, VMEM, HBM) + ((HBM,) if keep else ()),
        scratch_shapes=[
            ring,
            sums,
            flat,
            pltpu.VMEM((steps * width, ROWS, BLK), bf16),
            flat,
            table,
            square,
            results,
            pltpu.VMEM((peers, 2 * slots, HALF), f32),
            flat,
            pltpu.SemaphoreType.DMA((2,)),
            pltpu.SemaphoreType.DMA((2,)),
        ]
        + ([ring_sems] if keep else []),
        compiler_params=params(48),
        name="cross",
    )(plan, chosen, received, near, total, sens)
    received2 = lax.all_to_all(payload2, AXES, split_axis=0, concat_axis=0, tiled=True)
    back = pl.pallas_call(
        functools.partial(back_local_kernel, BACK),
        out_shape=shape((blocks, ROWS, BLK), f32),
        in_specs=[HBM, HBM, VMEM, HBM],
        out_specs=VMEM,
        scratch_shapes=[
            row,
            row,
            pltpu.VMEM((blocks + pairs, BLK, BLK), bf16),
            pltpu.SemaphoreType.DMA((2,)),
            pltpu.SemaphoreType.DMA(((blocks + pairs) // LOAD,)),
        ],
        compiler_params=params(48),
        cost_estimate=pl.CostEstimate(
            flops=(blocks + pairs) * BLK * BLK * 100, bytes_accessed=1 << 20, transcendentals=0
        ),
        name="back_local",
    )(local_first, local_second, ratio, in_hbm(tiles))
    received2 = received2.reshape(places * 2, HALF)
    common = [sums, flat, pltpu.VMEM((places, BLK, BLK), bf16) if keep else ring]
    if keep:
        kernel, operands, specs = back_cross_kernel, (in_hbm(cross_tiles[0]),), [HBM]
        kernel = functools.partial(kernel, BACK, peers - 1)
        scratch = [pltpu.SMEM((1 + 2 * longest,), i32), pltpu.SemaphoreType.DMA((2,)), pltpu.SemaphoreType.DMA((places // LOAD,))]
    else:
        kernel, operands, specs = back_again_kernel, (received, near), [VMEM, VMEM]
        scratch = [square, pltpu.VMEM((steps * width, 1, BLK), f32), pltpu.SemaphoreType.DMA((1,))]
        kernel = functools.partial(kernel, width, slots)
    sensitivity = pl.pallas_call(
        kernel,
        out_shape=shape((flat_rows, HALF), f32),
        in_specs=[pl.BlockSpec(memory_space=pl.ANY) if keep else SMEM, VMEM, *specs, VMEM, HBM],
        out_specs=VMEM,
        scratch_shapes=common + scratch,
        compiler_params=params(48),
        name="back_cross",
    )(plan, received2, *operands, back, vol)
    return (filtered.reshape(-1), sensitivity.reshape(-1))


def solution(mesh):
    return jax.shard_map(
        shards,
        mesh=mesh,
        in_specs=(
            P(None, AXES),
            P(AXES),
            P(AXES),
            P(AXES),
            P(AXES),
            P(AXES),
            P(AXES, None),
            P(AXES, None, None),
        ),
        out_specs=(P(AXES), P(AXES)),
        check_vma=False,
    )
```

```python
import functools

import jax
import jax.numpy as jnp
from jax import lax
from jax.experimental import pallas as pl
from jax.experimental.pallas import tpu as pltpu
from jax.sharding import PartitionSpec as P

BLK = 256
HALF = BLK // 2
AXES = ("px", "py")
ROWS = 8
WORDS = 5
PEER_ROWS = 24
FEATURES = 32
COORD = 16384.0
VOLUME = 21845.0
DENSITY = 65535.0
MIDDLE = 1.5
TINY = 4e-6
BACK = 16
LOAD = 4
WIDTH = 1
LOOK = 3
DEPTH = 12
KEEP_LIMIT = 20 << 20
MIB = 1 << 20

VMEM = pl.BlockSpec(memory_space=pltpu.VMEM)
SMEM = pl.BlockSpec(memory_space=pltpu.SMEM)
HBM = pl.BlockSpec(memory_space=pltpu.HBM)


def fixed(value, steps):
    return (value * steps + 0.5).astype(jnp.int32)


def two_halves(first, second):
    return first | (second << 16)


def pack_kernel(chosen_in, cent_in, vol_in, dens_in, payload, words, chosen, cent, vol, dens, sends, sems, out_sems):
    blocks = words.shape[0]
    waits = fetch(
        [(cent_in, cent), (vol_in, vol), (dens_in, dens), (chosen_in, chosen)], sems
    )
    words[...] = jnp.zeros_like(words)
    for wait in waits:
        wait()
    for b in range(blocks):
        low = cent[:, b * BLK : b * BLK + HALF]
        high = cent[:, b * BLK + HALF : (b + 1) * BLK]
        words[b, 0:3, :] = two_halves(fixed(low, COORD), fixed(high, COORD))
    for row, source, steps in ((3, vol, VOLUME), (4, dens, DENSITY)):
        low = source[pl.ds(0, blocks, stride=2), :]
        high = source[pl.ds(1, blocks, stride=2), :]
        words[:, row, :] = two_halves(fixed(low, steps), fixed(high, steps))
    slots, peers = chosen.shape

    def send(p, carry):
        for s in range(slots):
            sends[p, WORDS * s : WORDS * (s + 1), :] = words[chosen[s, p], 0:WORDS, :]
        return carry

    chunks = out_sems.shape[0]
    share = peers // chunks
    copies = []
    for c in range(chunks):
        lax.fori_loop(c * share, (c + 1) * share, send, 0, unroll=4)
        part = pl.ds(c * share, share)
        copies.append(pltpu.make_async_copy(sends.at[part], payload.at[part], out_sems.at[c]))
        copies[-1].start()
    for copy in copies:
        copy.wait()


def decode(word):
    row = lax.broadcasted_iota(jnp.int32, (ROWS, BLK), 0)
    step = jnp.where(
        row < 3,
        1.0 / COORD,
        jnp.where(row == 3, 1.0 / VOLUME, jnp.where(row == 4, 1.0 / DENSITY, 0.0)),
    )
    parts = jnp.concatenate([word & 0xFFFF, lax.shift_right_logical(word, 16)], axis=1)
    held = parts.astype(jnp.float32) * step
    volume = held[3:4, :]
    values = jnp.where(row == 4, held * volume, held).astype(jnp.bfloat16)
    place = jnp.where(row < 3, held - MIDDLE, 0.0)
    high = place.astype(jnp.bfloat16).astype(jnp.float32)
    low = place - high
    norm = jnp.sum(place * place, axis=0, keepdims=True)
    norm1 = norm.astype(jnp.bfloat16).astype(jnp.float32)
    rest = norm - norm1
    norm2 = rest.astype(jnp.bfloat16).astype(jnp.float32)
    norm3 = rest - norm2
    one = jnp.where(row == 6, 1.0, 0.0)
    far1 = high + jnp.where(
        row == 3, norm1, jnp.where(row == 4, norm2, jnp.where(row == 5, norm3, one))
    )
    far2 = low + jnp.where((row == 3) | (row == 4), 1.0, 0.0)
    far = jnp.concatenate([far1, far2], axis=0).astype(jnp.bfloat16)
    far = jnp.concatenate([far, far], axis=0)
    near1 = -2.0 * high + jnp.where(
        (row >= 3) & (row <= 5), 1.0, jnp.where(row == 6, norm1, 0.0)
    )
    near2 = -2.0 * high + jnp.where(row == 3, norm2, jnp.where(row == 4, norm3, 0.0))
    near34 = -2.0 * low
    near = jnp.concatenate([near1, near2, near34, near34], axis=0).astype(jnp.bfloat16)
    return far, near, values


def product(rows, tile):
    return jnp.dot(rows, tile, preferred_element_type=jnp.float32)


def product_t(rows, tile):
    return lax.dot_general(
        rows, tile, (((1,), (1,)), ((), ())), preferred_element_type=jnp.float32
    )


def cone(squares, u):
    root = squares[u] * lax.rsqrt(jnp.maximum(squares[u], TINY))
    return jnp.maximum((1.0 - root).astype(jnp.bfloat16), 0)


def staged(groups, peel, width, tiles, kept, sems, squares, results, square, use, settle, beside=None):
    def place(d, u):
        return d % DEPTH * width + u

    def copy(k, count):
        part = pl.ds(k * DEPTH * width, count * width)
        return pltpu.make_async_copy(tiles.at[part], kept.at[part], sems.at[k])

    slots = LOOK + 1

    def distances(g, d):
        for u in range(width):
            squares[(d % slots) * width + u] = square(g * width + u, place(d, u))

    def cones(view, d):
        for u in range(width):
            view[d * width + u] = cone(squares, (d % slots) * width + u)

    def sums(view, g, d):
        for u in range(width):
            parts = use(g * width + u, place(d, u), view[d * width + u])
            for result, part in zip(results, parts):
                result[d * width + u] = part

    def settled(g, count):
        for d in range(count):
            for u in range(width):
                settle((g + d) * width + u, d * width + u)

    def view_from(g, count):
        return tiles.at[pl.ds(g * width, count * width)]

    for d in range(slots):
        distances(d, d)
    cones(view_from(0, 1), 0)
    turns = (groups - slots - peel) // DEPTH

    def steps(g, count):
        view = view_from(g, count + 1)
        for d in range(count):
            sums(view, g + d, d)
            distances(g + d + slots, d + slots)
            cones(view, d + 1)
        settled(g, count)

    def turn(k, carry):
        if beside is not None:
            beside(k)
        steps(k * DEPTH, DEPTH)
        if kept is not None:
            copy(k, DEPTH).start()
        return carry

    lax.fori_loop(0, turns, turn, 0)
    g = turns * DEPTH
    last = peel + slots
    view = view_from(g, last)
    for d in range(last):
        sums(view, g + d, d)
        if d < peel:
            distances(g + d + slots, d + slots)
        if d + 1 < last:
            cones(view, d + 1)
    if kept is not None:
        copy(turns, last).start()
    settled(g, last)

    def wait():
        def one(k, carry):
            copy(k, DEPTH).wait()
            return carry

        lax.fori_loop(0, turns, one, 0)
        copy(turns, last).wait()

    return wait


def peeled(most):
    return (most - LOOK - 1) % DEPTH


def padded(groups, peel):
    least = LOOK + 1 + peel
    return jnp.maximum((groups - least + DEPTH - 1) // DEPTH, 0) * DEPTH + least


def chunked(size, room, width, ring, squares, results, square, use, settle):
    def chunk(c, carry):
        base = c * room
        left = jnp.minimum(size - base, room)
        staged(
            padded((left + width - 1) // width, 0),
            0,
            width,
            ring,
            None,
            None,
            squares,
            results,
            lambda i, at: square(base + i, at),
            lambda i, at, tile: use(base + i, at, tile),
            lambda i, at: settle(jnp.where(i < left, base + i, size), at),
        )
        return carry

    lax.fori_loop(0, jnp.maximum((size + room - 1) // room, 1), chunk, 0)


def fetch(pairs, sems):
    copies = [pltpu.make_async_copy(a, b, sems.at[k]) for k, (a, b) in enumerate(pairs)]
    for copy in copies:
        copy.start()
    return [copy.wait for copy in copies]


def local_kernel(
    width, first_in, second_in, counts_in, chosen_in, words, total, kept, near, plan,
    first, second, counts, chosen, ring, far_t, vals, squares, sums0, sums1, sems, self_sems, pair_sems,
):
    blocks = words.shape[0]
    pairs = first.shape[0]
    peers = counts.shape[1]
    slots = chosen.shape[0]
    waits = fetch(
        [(first_in, first), (second_in, second), (counts_in, counts), (chosen_in, chosen)], sems
    )

    def square_self(b, at):
        f, n, v = decode(words[b])
        f = f.T
        far_t[b] = f
        near[b] = n
        vals[b] = v
        return product(f, n)

    def use_self(b, at, tile):
        return (product(vals[b], tile),)

    def settle_self(b, at):
        total[b] = sums0[at]

    part = pl.ds(0, blocks)
    wait_self = staged(
        blocks // width, peeled(blocks // width), width, ring.at[part], kept.at[part], self_sems, squares, (sums0,),
        square_self, use_self, settle_self,
    )
    for wait in waits:
        wait()

    def square_pair(j, at):
        return product(far_t[second[j]], near[first[j]])

    def use_pair(j, at, tile):
        return product(vals[second[j]], tile), product_t(vals[first[j]], tile)

    def settle_pair(j, at):
        total[first[j]] += sums0[at]
        total[second[j]] += sums1[at]

    length = plan_length(plan)
    turns = (pairs // width - LOOK - 1) // DEPTH
    share = -(-peers // turns)
    plan[0] = 0

    def collect(k):
        found = plan[0]
        for q in range(share):
            p = k * share + q
            peer = jnp.minimum(p, peers - 1)
            count = jnp.where(p < peers, counts[0, peer], 0)
            for s in range(slots):
                plan[1 + found] = peer * slots + s
                plan[1 + length + found] = chosen[s, peer]
                found = found + (s < count).astype(jnp.int32)
        plan[0] = found

    part = pl.ds(blocks, pairs)
    wait_pair = staged(
        pairs // width, peeled(pairs // width), width, ring.at[part], kept.at[part], pair_sems, squares, (sums0, sums1),
        square_pair, use_pair, settle_pair, collect,
    )

    for i in range(2 * DEPTH * width):
        plan[1 + plan[0] + i] = 0
        plan[1 + length + plan[0] + i] = 0
    wait_self()
    wait_pair()


def plan_length(plan):
    return (plan.shape[0] - 1) // 2


def far_word(received, slots, place):
    peer, slot = place // slots, place % slots
    return received[pl.ds(peer * PEER_ROWS + slot * WORDS, ROWS), :]


def cross_kernel(
    width, keep, plan, chosen_in, received, near, total_in, sens_in, filtered, ratio, payload, *rest
):
    kept = None
    if keep:
        kept, *rest = rest
    ring, total, flat, vals, sens, chosen, squares, sums0, sends, filts, sems, out_sems, *ring_sems = rest
    blocks = near.shape[0]
    waits = fetch([(chosen_in, chosen), (sens_in, sens)], sems)
    total[...] = total_in[...]
    slots, peers = chosen.shape
    size, length = plan[0], plan_length(plan)

    def square(i, at):
        f, unused, v = decode(far_word(received, slots, plan[1 + i]))
        vals[at] = v
        return product(f.T, near[plan[1 + length + i]])

    def use(i, at, tile):
        return (product(vals[at], tile),)

    def settle(i, at):
        total[plan[1 + length + i]] += jnp.where(i < size, sums0[at], 0.0)

    if keep:
        peel = peeled((peers - 1) * slots // width)
        groups = padded((size + width - 1) // width, peel)
        wait_tiles = staged(
            groups, peel, width, ring, kept, ring_sems[0], squares, (sums0,), square, use, settle
        )
    else:
        room = ring.shape[0] - (DEPTH + LOOK + 1) * width
        chunked(size, room, width, ring, squares, (sums0,), square, use, settle)
    for wait in waits:
        wait()
    base = total[:, 3, :]
    for half in range(2):
        rows = pl.ds(half, blocks, stride=2)
        part = sens[rows, :] / base[:, half * HALF : (half + 1) * HALF]
        flat[rows, :] = part.astype(jnp.bfloat16).astype(jnp.float32)

    def send(p, carry):
        for s in range(slots):
            sends[p, 2 * s : 2 * s + 2, :] = flat[pl.ds(2 * chosen[s, p], 2), :]
        return carry

    lax.fori_loop(0, peers, send, 0, unroll=4)
    sent = pltpu.make_async_copy(sends, payload, out_sems.at[0])
    sent.start()
    filt = total[:, 4, :] / base
    ratio[...] = jnp.zeros_like(ratio)
    for half in range(2):
        rows = pl.ds(half, blocks, stride=2)
        lanes = slice(half * HALF, (half + 1) * HALF)
        filts[rows, :] = filt[:, lanes]
        ratio[:, 0, lanes] = flat[rows, :]
    written = pltpu.make_async_copy(filts, filtered, out_sems.at[1])
    written.start()
    if keep:
        wait_tiles()
    sent.wait()
    written.wait()


def tile_loads(width, kept, tiles, sems):
    each = width // LOAD

    def copy(k):
        part = pl.ds(k * LOAD, LOAD)
        return pltpu.make_async_copy(kept.at[part], tiles.at[part], sems.at[k])

    def start(a, b):
        def one(k, carry):
            copy(k).start()
            return carry

        lax.fori_loop(a * each, b * each, one, 0)

    def ready(k):
        for j in range(each):
            copy(k * each + j).wait()

    return start, ready


def back_local_kernel(
    width, first_in, second_in, ratio, kept, total, first, second, tiles, sems, tile_sems
):
    blocks = ratio.shape[0]
    pairs = first.shape[0]
    start, ready = tile_loads(width, kept, tiles, tile_sems)
    waits = fetch([(first_in, first), (second_in, second)], sems)
    start(blocks // width, (blocks + pairs) // width)
    start(0, blocks // width)
    total[...] = jnp.zeros_like(total)

    def rows(b):
        return ratio[b].astype(jnp.bfloat16)

    for wait in waits:
        wait()

    def pair(k, carry):
        ready(blocks // width + k)
        ids = [(first[k * width + u], second[k * width + u]) for u in range(width)]
        sums = []
        for u, (a, b) in enumerate(ids):
            tile = tiles[blocks + k * width + u]
            sums.append((product(rows(b), tile), product_t(rows(a), tile)))
        for (a, b), (to_first, to_second) in zip(ids, sums):
            total[a] += to_first
            total[b] += to_second
        return carry

    lax.fori_loop(0, pairs // width, pair, 0)

    def own(k, carry):
        ready(k)
        sums = [product(rows(k * width + u), tiles[k * width + u]) for u in range(width)]
        for u in range(width):
            total[k * width + u] += sums[u]
        return carry

    lax.fori_loop(0, blocks // width, own, 0)


def far_ratio(ratio, place):
    row0 = ratio[pl.ds(place * 2, 1), :]
    row1 = ratio[pl.ds(place * 2 + 1, 1), :]
    return jnp.concatenate([row0, row1], axis=1).astype(jnp.bfloat16)


def finish_back(blocks, vol, total, out):
    for half in range(2):
        rows = pl.ds(half, blocks, stride=2)
        lanes = slice(half * HALF, (half + 1) * HALF)
        out[rows, :] = vol[rows, :] * total[:, 0, lanes]


def back_cross_kernel(
    width, least, plan_in, ratio, kept, total_in, vol_in, out,
    total, vol, tiles, plan, sems, tile_sems,
):
    blocks = total.shape[0]
    start, ready = tile_loads(width, kept, tiles, tile_sems)
    wait_plan, *waits = fetch([(plan_in, plan), (vol_in, vol)], sems)
    early = -(-least // width)
    start(0, early)
    total[...] = total_in[...]
    wait_plan()
    size, length = plan[0], plan_length(plan)
    groups = (size + width - 1) // width
    start(early, groups)

    def turn(k, carry):
        ready(k)
        sums = []
        for u in range(width):
            i = k * width + u
            part = product(far_ratio(ratio, plan[1 + i]), tiles[i])
            part = jnp.where(i < size, part, 0.0)
            sums.append((plan[1 + length + i], part))
        for b, part in sums:
            total[b, 0:1, :] += part
        return carry

    lax.fori_loop(0, groups, turn, 0)
    for wait in waits:
        wait()
    finish_back(blocks, vol, total, out)


def back_again_kernel(
    width, slots, plan, ratio, received, near, total_in, vol_in, out,
    total, vol, ring, squares, sums0, sems,
):
    blocks = total.shape[0]
    waits = fetch([(vol_in, vol)], sems)
    total[...] = total_in[...]
    size, length = plan[0], plan_length(plan)

    def square(i, at):
        f, unused, v = decode(far_word(received, slots, plan[1 + i]))
        return product(f.T, near[plan[1 + length + i]])

    def use(i, at, tile):
        return (product(far_ratio(ratio, plan[1 + i]), tile),)

    def settle(i, at):
        total[plan[1 + length + i], 0:1, :] += jnp.where(i < size, sums0[at], 0.0)

    room = ring.shape[0] - (DEPTH + LOOK + 1) * width
    chunked(size, room, width, ring, squares, (sums0,), square, use, settle)
    for wait in waits:
        wait()
    finish_back(blocks, vol, total, out)


def in_hbm(array):
    return pltpu.with_memory_space_constraint(array, pltpu.HBM)


def params(mib):
    return pltpu.CompilerParams(vmem_limit_bytes=mib * MIB)


def shards(
    centroids, volumes, densities, sens_in, local_first, local_second, pair_count, pair_mine
):
    elements = volumes.shape[0]
    blocks = elements // BLK
    flat_rows = elements // HALF
    vol = in_hbm(volumes.reshape(flat_rows, HALF))
    dens = in_hbm(densities.reshape(flat_rows, HALF))
    sens = in_hbm(sens_in.reshape(flat_rows, HALF))
    local_first, local_second = in_hbm(local_first), in_hbm(local_second)
    chosen = in_hbm(pair_mine[0].T)
    slots, peers = chosen.shape
    places = peers * slots
    pairs = local_first.shape[0]
    longest = 2 * places
    f32, bf16, i32 = jnp.float32, jnp.bfloat16, jnp.int32
    shape = jax.ShapeDtypeStruct
    width = WIDTH
    flat = pltpu.VMEM((flat_rows, HALF), f32)
    sums = pltpu.VMEM((blocks, ROWS, BLK), f32)
    square = pltpu.VMEM(((LOOK + 1) * width, BLK, BLK), f32)
    tile_bytes = BLK * BLK * 2
    keep = places * tile_bytes <= KEEP_LIMIT
    most = (places - slots) // width
    turns = most // DEPTH
    held = max(most * width, -(-most * width // BACK) * BACK)
    ring = pltpu.VMEM((held if keep else KEEP_LIMIT // tile_bytes, BLK, BLK), bf16)
    steps = DEPTH + LOOK + 1
    results = pltpu.VMEM((steps * width, ROWS, BLK), f32)
    ring_sems = pltpu.SemaphoreType.DMA((turns + 1,))
    table = pltpu.SMEM(chosen.shape, i32)
    row = pltpu.SMEM((pairs,), i32)

    payload, words = pl.pallas_call(
        pack_kernel,
        out_shape=(pltpu.HBM((peers, PEER_ROWS, HALF), i32), shape((blocks, ROWS, HALF), i32)),
        in_specs=[HBM] * 4,
        out_specs=(HBM, VMEM),
        scratch_shapes=[
            table,
            pltpu.VMEM(centroids.shape, f32),
            flat,
            flat,
            pltpu.VMEM((peers, PEER_ROWS, HALF), i32),
            pltpu.SemaphoreType.DMA((4,)),
            pltpu.SemaphoreType.DMA((4,)),
        ],
        compiler_params=params(8),
        name="pack",
    )(chosen, in_hbm(centroids), vol, dens)
    received = lax.all_to_all(payload, AXES, split_axis=0, concat_axis=0, tiled=True)
    total, tiles, near, plan = pl.pallas_call(
        functools.partial(local_kernel, width),
        out_shape=(
            shape((blocks, ROWS, BLK), f32),
            pltpu.HBM((blocks + pairs, BLK, BLK), bf16),
            shape((blocks, FEATURES, BLK), bf16),
            shape((1 + 2 * longest,), i32),
        ),
        in_specs=[HBM, HBM, HBM, HBM, VMEM],
        out_specs=(VMEM, HBM, VMEM, SMEM),
        scratch_shapes=[
            row,
            row,
            pltpu.SMEM(pair_count.shape, i32),
            table,
            pltpu.VMEM((blocks + pairs, BLK, BLK), bf16),
            pltpu.VMEM((blocks, BLK, FEATURES), bf16),
            pltpu.VMEM((blocks, ROWS, BLK), bf16),
            square,
            results,
            results,
            pltpu.SemaphoreType.DMA((4,)),
            pltpu.SemaphoreType.DMA((blocks // width // DEPTH + 1,)),
            pltpu.SemaphoreType.DMA((pairs // width // DEPTH + 1,)),
        ],
        compiler_params=params(48),
        cost_estimate=pl.CostEstimate(
            flops=(blocks + pairs) * BLK * BLK * 100, bytes_accessed=1 << 20, transcendentals=0
        ),
        name="local",
    )(local_first, local_second, in_hbm(pair_count), chosen, words)
    received = received.reshape(peers * PEER_ROWS, HALF)
    filtered, ratio, payload2, *cross_tiles = pl.pallas_call(
        functools.partial(cross_kernel, width, keep),
        out_shape=(
            pltpu.HBM((flat_rows, HALF), f32),
            shape((blocks, ROWS, BLK), f32),
            pltpu.HBM((peers, 2 * slots, HALF), f32),
        )
        + ((pltpu.HBM((held, BLK, BLK), bf16),) if keep else ()),
        in_specs=[SMEM, HBM, VMEM, VMEM, VMEM, HBM],
        out_specs=(HBM, VMEM, HBM) + ((HBM,) if keep else ()),
        scratch_shapes=[
            ring,
            sums,
            flat,
            pltpu.VMEM((steps * width, ROWS, BLK), bf16),
            flat,
            table,
            square,
            results,
            pltpu.VMEM((peers, 2 * slots, HALF), f32),
            flat,
            pltpu.SemaphoreType.DMA((2,)),
            pltpu.SemaphoreType.DMA((2,)),
        ]
        + ([ring_sems] if keep else []),
        compiler_params=params(48),
        name="cross",
    )(plan, chosen, received, near, total, sens)
    received2 = lax.all_to_all(payload2, AXES, split_axis=0, concat_axis=0, tiled=True)
    back = pl.pallas_call(
        functools.partial(back_local_kernel, BACK),
        out_shape=shape((blocks, ROWS, BLK), f32),
        in_specs=[HBM, HBM, VMEM, HBM],
        out_specs=VMEM,
        scratch_shapes=[
            row,
            row,
            pltpu.VMEM((blocks + pairs, BLK, BLK), bf16),
            pltpu.SemaphoreType.DMA((2,)),
            pltpu.SemaphoreType.DMA(((blocks + pairs) // LOAD,)),
        ],
        compiler_params=params(48),
        cost_estimate=pl.CostEstimate(
            flops=(blocks + pairs) * BLK * BLK * 100, bytes_accessed=1 << 20, transcendentals=0
        ),
        name="back_local",
    )(local_first, local_second, ratio, in_hbm(tiles))
    received2 = received2.reshape(places * 2, HALF)
    common = [sums, flat, pltpu.VMEM((places, BLK, BLK), bf16) if keep else ring]
    if keep:
        kernel, operands, specs = back_cross_kernel, (in_hbm(cross_tiles[0]),), [HBM]
        kernel = functools.partial(kernel, BACK, peers - 1)
        scratch = [pltpu.SMEM((1 + 2 * longest,), i32), pltpu.SemaphoreType.DMA((2,)), pltpu.SemaphoreType.DMA((places // LOAD,))]
    else:
        kernel, operands, specs = back_again_kernel, (received, near), [VMEM, VMEM]
        scratch = [square, pltpu.VMEM((steps * width, 1, BLK), f32), pltpu.SemaphoreType.DMA((1,))]
        kernel = functools.partial(kernel, width, slots)
    sensitivity = pl.pallas_call(
        kernel,
        out_shape=shape((flat_rows, HALF), f32),
        in_specs=[pl.BlockSpec(memory_space=pl.ANY) if keep else SMEM, VMEM, *specs, VMEM, HBM],
        out_specs=VMEM,
        scratch_shapes=common + scratch,
        compiler_params=params(48),
        name="back_cross",
    )(plan, received2, *operands, back, vol)
    return (filtered.reshape(-1), sensitivity.reshape(-1))


def solution(mesh):
    return jax.shard_map(
        shards,
        mesh=mesh,
        in_specs=(
            P(None, AXES),
            P(AXES),
            P(AXES),
            P(AXES),
            P(AXES),
            P(AXES),
            P(AXES, None),
            P(AXES, None, None),
        ),
        out_specs=(P(AXES), P(AXES)),
        check_vma=False,
    )
```
